128 devices in a mesh: row: 16 (over y, x), col: 8 (over z, core).
Axes of the slice: x: 4, y: 4, z: 4, core: 2. Of those that a mesh axis runs over, the one named last changes fastest.
Arguments:
- child_blocks: float32 [16384, 8192], P('row', 'col'), as said below
- block_map: int32 [2, 64], replicated, may hold values from 0 to 127, as said below
- front_diagonal: float32 [16384], replicated, may hold values from 40 to 80
Outputs:
- front: float32 [16384, 16384], P('row', 'col')
The draws below stay inside these ranges and needn't reach their ends.
Inputs may be any that keep to these rules, and one draw needn't show every extreme that they name: `child_blocks`: each child's block is symmetric: X_c transposed equals X_c. Each panel's pivot block front[K, K], as it stands before panel k, is symmetric positive definite. For each child the 64 entries of block_map[c] are distinct. Split them into 8 aligned groups of 8 in order: each group names exactly 1 block in every range of 16 consecutive parent blocks starting at a multiple of 16, and at most 1 in every such range of 8; for each child some range of 8 gets exactly 1 from every group.
All inputs are finite; a program needn't handle non-finite values.
Results may differ from the reference program's by a relative error of at most 0.0001.
Values sent between devices are 32-bit elements; how exact they have to be, the bound alone decides.
A program may use at most 128 MiB of HBM per device.

```python
import math
import jax
import jax.numpy as jnp
from jax import lax

F = 16384
C = 8192
BLK = 128
PW = 512
NBC = 64
NGROUP = 8
SBC = 8
KC = 1
KR = 1
BPR = 8


def draw_child_blocks(key, part):
    key = jax.random.fold_in(key, 5)
    raw_values = jax.random.normal(key, (2, C, C), jnp.float32)
    sym_part = (raw_values + jnp.swapaxes(raw_values, 1, 2)) * (40.0 / math.sqrt(2.0 * C))
    return sym_part.reshape(2 * C, C)


def draw_block_map(key, part):
    key = jax.random.fold_in(key, 11)
    key_pick, key_star, key_order, key_slot = jax.random.split(key, 4)
    option_count = 2 * KR
    option_ids = jnp.arange(option_count, dtype=jnp.int32)
    scores = jax.random.randint(key_pick, (2, NGROUP, NGROUP, option_count), 0, 1 << 20) * option_count + option_ids
    star_range = jax.random.randint(key_star, (2, 1, 1, 1), 0, NGROUP)
    star_side = jax.random.randint(jax.random.fold_in(key_star, 1), (2, 1, 1, 1), 0, 2)
    favoured = (jnp.arange(NGROUP, dtype=jnp.int32)[None, None, :, None] == star_range) & ((option_ids // KR)[None, None, None, :] == star_side)
    scores = scores + jnp.where(favoured, 1 << 28, 0)
    top_scores, chosen = lax.top_k(scores, KC)
    side_ids = chosen.astype(jnp.int32) // KR
    range_ids = 2 * jnp.arange(NGROUP, dtype=jnp.int32)[None, None, :, None] + side_ids
    listed = range_ids.reshape(2, NGROUP, SBC)
    order_keys = jax.random.randint(key_order, (2, NGROUP, SBC), 0, 1 << 20) * SBC + jnp.arange(SBC, dtype=jnp.int32)
    ordering = jnp.argsort(order_keys, axis=-1).astype(jnp.int32)
    placed = jnp.take_along_axis(listed, ordering, axis=-1).reshape(2, NBC)
    matches = (placed[:, :, None] == jnp.arange(2 * NGROUP, dtype=jnp.int32)[None, None, :]).astype(jnp.int32)
    earlier = jnp.cumsum(matches, axis=1) - matches
    rank_ids = jnp.sum(earlier * matches, axis=2)
    slot_keys = jax.random.randint(key_slot, (2, 2 * NGROUP, BPR), 0, 1 << 20) * BPR + jnp.arange(BPR, dtype=jnp.int32)
    shuffled = jnp.argsort(slot_keys, axis=-1).astype(jnp.int32)
    within = jnp.take_along_axis(shuffled.reshape(2, 2 * NGROUP * BPR), placed * BPR + rank_ids, axis=1)
    return (placed * BPR + within).astype(jnp.int32)


def setup_inputs(seed: int = 0) -> dict:
    key_of = jax.random.split(jax.random.key(seed), 4)
    return {
        "child_blocks": draw_child_blocks(jax.random.fold_in(key_of[3], 71), 0),
        "block_map": draw_block_map(jax.random.fold_in(key_of[3], 71), 0),
        "front_diagonal": jnp.clip(jax.random.uniform(key_of[2], (F,), jnp.float32, 40.0, 80.0), 40.0, 80.0),
    }


def reference(child_blocks, block_map, front_diagonal):
    front = jnp.diag(front_diagonal).astype(jnp.float32)
    offsets = jnp.arange(BLK, dtype=jnp.int32)
    for child_index in range(2):
        positions = (block_map[child_index][:, None] * BLK + offsets[None, :]).reshape(-1).astype(jnp.int32)
        contribution = child_blocks[child_index * C:(child_index + 1) * C]
        spread = jnp.zeros((F, C), jnp.float32).at[positions].set(contribution)
        front = front.at[:, positions].add(spread)
    for panel_index in range(2):
        start_col = panel_index * PW
        end_col = start_col + PW
        pivot_block = front[start_col:end_col, start_col:end_col]
        lower_block = front[end_col:, start_col:end_col]
        factor = jnp.linalg.solve(pivot_block.T, lower_block.T).T
        upper_block = front[start_col:end_col, end_col:]
        update = jnp.dot(factor.astype(jnp.float32), upper_block.astype(jnp.float32), precision=lax.Precision.HIGHEST, preferred_element_type=jnp.float32)
        front = front.at[end_col:, start_col:end_col].set(factor)
        front = front.at[end_col:, end_col:].add(-update)
    return front
```

```python
import jax
import jax.numpy as jnp
from jax import lax
from jax.experimental import pallas as pl
from jax.experimental.pallas import tpu as pltpu
from jax.sharding import PartitionSpec as P

BLK = 128
PW = 512
TR = 1024
TC = 2048
MESH = pl.DeviceIdType.MESH
VMEM_LIMIT = 56 * 1024 * 1024
ANY = pl.BlockSpec(memory_space=pl.ANY)
SMEM = pl.BlockSpec(memory_space=pltpu.SMEM)
VMEM = pl.BlockSpec(memory_space=pltpu.VMEM)


def pack_kernel(map_ref, child_ref, send_ref, table_ref, sem):
    row, col = lax.axis_index("row"), lax.axis_index("col")
    child, group = row // 8, row % 8

    def start(step, carry):
        t, u = step // 8, step % 8
        q = map_ref[child, group * 8 + t] // 16
        c = map_ref[child, col * 8 + u] // 16
        pltpu.make_async_copy(
            child_ref.at[
                pl.ds(pl.multiple_of(t * BLK, BLK), BLK), pl.ds(pl.multiple_of(u * BLK, BLK), BLK)
            ],
            send_ref.at[q * 8 + c],
            sem,
        ).start()
        return carry

    lax.fori_loop(0, 64, start, 0)

    def clear(step, carry):
        table_ref[step // 32, step % 32] = -1
        return carry

    lax.fori_loop(0, 64, clear, 0)

    def look(step, carry):
        k, s = step // 64, step % 64
        b = map_ref[k, s]

        @pl.when(b // 8 == row)
        def _():
            table_ref[k, b % 8] = s // 8

        @pl.when(b // 16 == col)
        def _():
            table_ref[k, 8 + b % 16] = s // 8

        @pl.when(b < 8)
        def _():
            table_ref[k, 24 + b] = s // 8

        return carry

    lax.fori_loop(0, 128, look, 0)
    pltpu.make_async_copy(send_ref, send_ref, sem).wait()


def pack(block_map, child):
    return pl.pallas_call(
        pack_kernel,
        out_shape=(
            jax.ShapeDtypeStruct((64, BLK, BLK), jnp.float32),
            jax.ShapeDtypeStruct((2, 32), jnp.int32),
        ),
        in_specs=[SMEM, ANY],
        out_specs=(ANY, SMEM),
        scratch_shapes=[pltpu.SemaphoreType.DMA],
        name="pack",
    )(block_map, child)


def exchange_kernel(
    send_ref, recv_ref, strip_ref, main_s, main_r, col_s, col_r, own_sem, gat_s, gat_r
):
    row, col = lax.axis_index("row"), lax.axis_index("col")
    me = row * 8 + col
    x, y = row % 4, row // 4

    own_a = pltpu.make_async_copy(send_ref.at[(row // 2) * 8 + col], recv_ref.at[me], own_sem.at[0])
    own_b = pltpu.make_async_copy(send_ref.at[col * 8], strip_ref.at[y, x, col], own_sem.at[1])
    own_a.start()
    own_b.start()

    def send_strip(step, carry):
        to = (col + step) % 8
        pltpu.make_async_remote_copy(
            send_ref.at[to * 8], strip_ref.at[y, x, col], col_s, col_r,
            device_id=(row, to), device_id_type=MESH,
        ).start()
        return carry

    lax.fori_loop(1, 8, send_strip, 0)

    def send_block(step, carry):
        to = (me + step * 45) % 128
        to_row, to_col = to // 8, to % 8
        pltpu.make_async_remote_copy(
            send_ref.at[(to_row // 2) * 8 + to_col], recv_ref.at[me], main_s, main_r,
            device_id=(to_row, to_col), device_id_type=MESH,
        ).start()
        return carry

    xp, xm = y * 4 + (x + 1) % 4, y * 4 + (x + 3) % 4
    yp, ym = ((y + 1) % 4) * 4 + x, ((y + 3) % 4) * 4 + x
    xl, xr = (x + 3) % 4, (x + 1) % 4
    yl, yr = (y + 3) % 4, (y + 1) % 4

    def hop(index, piece, to_row):
        ref = strip_ref.at[piece]
        return pltpu.make_async_remote_copy(
            ref, ref, gat_s.at[index], gat_r.at[index],
            device_id=(to_row, col), device_id_type=MESH,
        )

    def landed(index, piece):
        ref = strip_ref.at[piece]
        pltpu.make_async_remote_copy(
            ref, ref, gat_s.at[index], gat_r.at[index],
            device_id=(row, col), device_id_type=MESH,
        ).wait_recv()

    lo, hi = pl.ds(0, 4), pl.ds(4, 4)
    two = [pl.ds(2 * i, 2) for i in range(4)]
    every = pl.ds(0, 4)

    seven = strip_ref.at[y, x, pl.ds(0, 7)]
    pltpu.make_async_remote_copy(
        seven, seven, col_s, col_r, device_id=(row, col), device_id_type=MESH
    ).wait()
    own_b.wait()

    hops = []

    def go(index, piece, to_row):
        copy = hop(index, piece, to_row)
        copy.start()
        hops.append(copy)

    go(0, (y, x, lo), xp)
    go(1, (y, x, lo), xm)
    go(2, (y, x, hi), yp)
    go(3, (y, x, hi), ym)
    lax.fori_loop(1, 32, send_block, 0)
    landed(0, (y, xl, lo))
    go(4, (y, xl, two[0]), xp)
    landed(1, (y, xr, lo))
    go(5, (y, xr, two[1]), xm)
    landed(2, (yl, x, hi))
    go(6, (yl, x, two[2]), yp)
    landed(3, (yr, x, hi))
    go(7, (yr, x, two[3]), ym)
    lax.fori_loop(32, 64, send_block, 0)
    xo, yo = (x + 2) % 4, (y + 2) % 4
    landed(4, (y, xo, two[0]))
    landed(5, (y, xo, two[1]))
    go(8, (y, every, lo), yp)
    go(9, (y, every, lo), ym)
    landed(6, (yo, x, two[2]))
    landed(7, (yo, x, two[3]))
    go(10, (every, x, hi), xp)
    go(11, (every, x, hi), xm)
    lax.fori_loop(64, 96, send_block, 0)
    first, last = pl.ds(0, 2), pl.ds(2, 2)
    landed(8, (yl, every, lo))
    go(12, (yl, first, lo), yp)
    landed(9, (yr, every, lo))
    go(13, (yr, last, lo), ym)
    landed(10, (every, xl, hi))
    go(14, (first, xl, hi), xp)
    landed(11, (every, xr, hi))
    go(15, (last, xr, hi), xm)
    lax.fori_loop(96, 128, send_block, 0)
    landed(12, (yo, first, lo))
    landed(13, (yo, last, lo))
    landed(14, (first, xo, hi))
    landed(15, (last, xo, hi))
    for copy in hops:
        copy.wait_send()
    own_a.wait()
    rest = recv_ref.at[pl.ds(0, 127)]
    pltpu.make_async_remote_copy(
        rest, rest, main_s, main_r, device_id=(row, col), device_id_type=MESH
    ).wait()


def exchange(send):
    dma = pltpu.SemaphoreType.DMA
    return pl.pallas_call(
        exchange_kernel,
        out_shape=(
            jax.ShapeDtypeStruct((128, BLK, BLK), jnp.float32),
            jax.ShapeDtypeStruct((4, 4, 8, BLK, BLK), jnp.float32),
        ),
        in_specs=[ANY],
        out_specs=(ANY, ANY),
        scratch_shapes=[dma, dma, dma, dma, dma((2,)), dma((16,)), dma((16,))],
        compiler_params=pltpu.CompilerParams(has_side_effects=True),
        name="exchange",
    )(send)


def split(value):
    high = value.astype(jnp.bfloat16)
    return high, (value - high.astype(jnp.float32)).astype(jnp.bfloat16)


def dot1(a, b):
    return jnp.dot(a, b, preferred_element_type=jnp.float32)


def dot3(a, b):
    return dot1(a[0], b[0]) + (dot1(a[0], b[1]) + dot1(a[1], b[0]))


def identity(n):
    return lax.broadcasted_iota(jnp.int32, (n, n), 0) == lax.broadcasted_iota(jnp.int32, (n, n), 1)


def inverse_into(matrix_ref, scaled_ref, x_ref, out_ref):
    eye = identity(PW)
    matrix = matrix_ref[...]
    diagonal = jnp.where(eye, matrix, 0.0)
    by_col = lax.rsqrt(jnp.sum(diagonal, axis=0, keepdims=True))
    by_row = lax.rsqrt(jnp.sum(diagonal, axis=1, keepdims=True))
    scaled = matrix * by_row * by_col
    scaled_ref[...] = scaled
    bound = jnp.max(jnp.sum(jnp.abs(scaled), axis=0, keepdims=True))
    alpha = jnp.minimum(1.0, 1.9 / bound)
    x_ref[...] = jnp.where(eye, 2.0 * alpha, 0.0) - alpha * alpha * scaled

    def body(carry):
        count, _ = carry
        value = split(x_ref[...])
        residual = jnp.where(eye, 1.0, 0.0) - dot3(split(scaled_ref[...]), value)
        x_ref[...] += dot3(value, split(residual))
        return count + 1, jnp.sum(residual * residual)

    lax.while_loop(
        lambda carry: (carry[0] < 48) & (carry[1] > 1e-6), body, (jnp.int32(0), jnp.float32(1.0))
    )
    residual = jnp.where(eye, 1.0, 0.0) - jnp.dot(
        scaled_ref[...], x_ref[...], precision=lax.Precision.HIGHEST, preferred_element_type=jnp.float32
    )
    value = x_ref[...]
    value = value + dot3(split(value), split(residual))
    out_ref[...] = value * by_row * by_col


def pivot_kernel(
    table_ref, diag_ref, recv_ref, strip_ref, y_ref, f_ref,
    strips, blocks, piv, tile, inv0, inv1, l10, scaled, newton, schur, sems,
):
    row, col = lax.axis_index("row"), lax.axis_index("col")

    @pl.when(col == 0)
    def _():
        load_a = pltpu.make_async_copy(strip_ref, strips, sems.at[0])
        load_b = pltpu.make_async_copy(recv_ref, blocks, sems.at[1])
        load_a.start()
        load_b.start()
        load_a.wait()

        def pivot_block(step, carry):
            a, b = step // 8, step % 8
            total = jnp.where(identity(BLK) & (a == b), diag_ref[pl.ds(a, 1), :], 0.0)
            for k in range(2):
                ga, gb = table_ref[k, 24 + a], table_ref[k, 24 + b]
                value = strips[k * 8 + jnp.maximum(ga, 0), jnp.maximum(gb, 0)]
                total = total + jnp.where((ga >= 0) & (gb >= 0), value, 0.0)
            piv[pl.ds(pl.multiple_of(a * BLK, BLK), BLK), pl.ds(pl.multiple_of(b * BLK, BLK), BLK)] = total
            return carry

        lax.fori_loop(0, 64, pivot_block, 0)
        schur[...] = piv[:PW, :PW]
        inverse_into(schur, scaled, newton, inv0)
        l10[...] = dot3(split(piv[PW:, :PW]), split(inv0[...]))
        schur[...] = piv[PW:, PW:] - dot3(split(l10[...]), split(piv[:PW, PW:]))

        load_b.wait()

        @pl.when(row == 0)
        def _():
            f_ref[:PW, :] = piv[:PW, :]
            f_ref[PW:, :PW] = l10[...]
            f_ref[PW:, PW:] = schur[...]
            y_ref[...] = jnp.zeros((TR, TR), jnp.float32)
            y_ref[PW:, :PW] = l10[...]

        @pl.when(row > 0)
        def _():
            inverse_into(schur, scaled, newton, inv1)

            def tile_block(step, carry):
                a, b = step // 8, step % 8
                total = jnp.zeros((BLK, BLK), jnp.float32)
                for k in range(2):
                    ga, hb = table_ref[k, a], table_ref[k, 24 + b]
                    value = blocks[k * 64 + jnp.maximum(ga, 0) * 8 + jnp.maximum(hb, 0)]
                    total = total + jnp.where((ga >= 0) & (hb >= 0), value, 0.0)
                tile[pl.ds(pl.multiple_of(a * BLK, BLK), BLK), pl.ds(pl.multiple_of(b * BLK, BLK), BLK)] = total
                return carry

            lax.fori_loop(0, 64, tile_block, 0)
            for part in range(2):
                rows = pl.ds(part * PW, PW)
                factor0 = dot3(split(tile[rows, :PW]), split(inv0[...]))
                f_ref[rows, :PW] = factor0
                rest = tile[rows, PW:] - dot3(split(factor0), split(piv[:PW, PW:]))
                factor1 = dot3(split(rest), split(inv1[...]))
                f_ref[rows, PW:] = factor1
                y_ref[rows, PW:] = factor1
                y_ref[rows, :PW] = f_ref[rows, :PW] - dot3(split(factor1), split(l10[...]))


def pivots(table, diag, recv, strips):
    f32 = jnp.float32
    half = pltpu.VMEM((PW, PW), f32)
    return pl.pallas_call(
        pivot_kernel,
        out_shape=(jax.ShapeDtypeStruct((TR, TR), f32), jax.ShapeDtypeStruct((TR, TR), f32)),
        in_specs=[SMEM, VMEM, ANY, ANY],
        out_specs=(VMEM, VMEM),
        scratch_shapes=[
            pltpu.VMEM((16, 8, BLK, BLK), f32),
            pltpu.VMEM((128, BLK, BLK), f32),
            pltpu.VMEM((TR, TR), f32),
            pltpu.VMEM((TR, TR), f32),
            half, half, half, half, half, half,
            pltpu.SemaphoreType.DMA((2,)),
        ],
        compiler_params=pltpu.CompilerParams(vmem_limit_bytes=VMEM_LIMIT),
        name="pivots",
    )(table, diag, recv, strips)


CHUNKS = 16


def spread_kernel(y_ref, out_ref, own_sem, ring_s, ring_r, core_s, core_r):
    row, col = lax.axis_index("row"), lax.axis_index("col")
    z, core = col // 2, col % 2
    size = TR // CHUNKS
    own = pltpu.make_async_copy(y_ref, out_ref, own_sem)

    def ring(source, t):
        step = 1 if t % 2 == 0 else 3
        rows = pl.ds(t * size, size)
        return pltpu.make_async_remote_copy(
            source.at[rows], out_ref.at[rows], ring_s.at[t], ring_r.at[t],
            device_id=(row, ((z + step) % 4) * 2), device_id_type=MESH,
        )

    def across(source, t):
        rows = pl.ds(t * size, size)
        return pltpu.make_async_remote_copy(
            source.at[rows], out_ref.at[rows], core_s.at[t], core_r.at[t],
            device_id=(row, z * 2 + 1), device_id_type=MESH,
        )

    @pl.when(col == 0)
    def _():
        own.start()
        for t in range(CHUNKS):
            ring(y_ref, t).start()
        for t in range(CHUNKS):
            across(y_ref, t).start()
        for t in range(CHUNKS):
            ring(y_ref, t).wait_send()
            across(y_ref, t).wait_send()
        own.wait()

    @pl.when((core == 0) & (z > 0))
    def _():
        for t in range(CHUNKS):
            ring(out_ref, t).wait_recv()
            end = 3 if t % 2 == 0 else 1

            @pl.when(z != end)
            def _():
                ring(out_ref, t).start()

            across(out_ref, t).start()
        for t in range(CHUNKS):
            end = 3 if t % 2 == 0 else 1

            @pl.when(z != end)
            def _():
                ring(out_ref, t).wait_send()

            across(out_ref, t).wait_send()

    @pl.when(core == 1)
    def _():
        for t in range(CHUNKS):
            across(out_ref, t).wait_recv()


def spread(y):
    dma = pltpu.SemaphoreType.DMA
    return pl.pallas_call(
        spread_kernel,
        out_shape=jax.ShapeDtypeStruct((TR, TR), jnp.float32),
        in_specs=[ANY],
        out_specs=ANY,
        scratch_shapes=[dma, dma((CHUNKS,)), dma((CHUNKS,)), dma((CHUNKS,)), dma((CHUNKS,))],
        compiler_params=pltpu.CompilerParams(has_side_effects=True),
        name="spread",
    )(y)


def update_kernel(table_ref, diag_ref, y_ref, f_ref, *refs):
    strips, blocks = refs[0:4], refs[4:8]
    out_ref, yh, yl, wh, wl = refs[8:]
    row, col = lax.axis_index("row"), lax.axis_index("col")
    step = pl.program_id(0)

    @pl.when(step == 0)
    def _():
        yh[...], yl[...] = split(y_ref[...])

    for u in range(2):
        j = step * 2 + u

        def strip_block(i, carry):
            on = identity(BLK) & (col * 16 + j == i)
            total = jnp.where(on, diag_ref[pl.ds(i, 1), :], 0.0)
            for k in range(2):
                g, h = table_ref[k, 24 + i], table_ref[k, 8 + j]
                value = strips[2 * u + k][0, 0, jnp.maximum(g, 0)]
                total = total + jnp.where((g >= 0) & (h >= 0), value, 0.0)
            at = pl.ds(pl.multiple_of(i * BLK, BLK), BLK)
            wh[pl.ds(u * BLK, BLK), at], wl[pl.ds(u * BLK, BLK), at] = split(total)
            return carry

        lax.fori_loop(0, 8, strip_block, 0)

    def nt(a, b):
        return lax.dot_general(a, b, (((1,), (1,)), ((), ())), preferred_element_type=jnp.float32)

    for part in range(2):
        rows = pl.ds(part * PW, PW)
        out_ref[rows, :] = -(nt(yh[rows, :], wh[...]) + (nt(yh[rows, :], wl[...]) + nt(yl[rows, :], wh[...])))

    for u in range(2):
        j = step * 2 + u

        def front_block(i, carry):
            on = identity(BLK) & (col * 16 + j == row * 8 + i)
            total = jnp.where(on, diag_ref[pl.ds(row * 8 + i, 1), :], 0.0)
            for k in range(2):
                g, h = table_ref[k, i], table_ref[k, 8 + j]
                value = blocks[2 * u + k][0, jnp.maximum(g, 0), 0]
                total = total + jnp.where((g >= 0) & (h >= 0), value, 0.0)
            out_ref[pl.ds(pl.multiple_of(i * BLK, BLK), BLK), pl.ds(u * BLK, BLK)] += total
            return carry

        lax.fori_loop(0, 8, front_block, 0)

    @pl.when((col == 0) & (step < 4))
    def _():
        out_ref[...] = f_ref[...]


def update(table, diag, y, factors, strips, recv):
    f32, bf16 = jnp.float32, jnp.bfloat16

    def strip_spec(u, k):
        return pl.BlockSpec(
            (1, 1, 8, BLK, BLK),
            lambda s, table: (k, jnp.maximum(table[k, 8 + 2 * s + u], 0), 0, 0, 0),
        )

    def block_spec(u, k):
        return pl.BlockSpec(
            (1, 8, 1, BLK, BLK),
            lambda s, table: (k, 0, jnp.maximum(table[k, 8 + 2 * s + u], 0), 0, 0),
        )

    pairs = [(u, k) for u in range(2) for k in range(2)]
    return pl.pallas_call(
        update_kernel,
        out_shape=jax.ShapeDtypeStruct((TR, TC), f32),
        grid_spec=pltpu.PrefetchScalarGridSpec(
            num_scalar_prefetch=1,
            grid=(8,),
            in_specs=[
                pl.BlockSpec((128, BLK), lambda s, table: (0, 0)),
                pl.BlockSpec((TR, TR), lambda s, table: (0, 0)),
                pl.BlockSpec((TR, 256), lambda s, table: (0, jnp.minimum(s, 3))),
                *[strip_spec(u, k) for u, k in pairs],
                *[block_spec(u, k) for u, k in pairs],
            ],
            out_specs=pl.BlockSpec((TR, 256), lambda s, table: (0, s)),
            scratch_shapes=[
                pltpu.VMEM((TR, TR), bf16),
                pltpu.VMEM((TR, TR), bf16),
                pltpu.VMEM((256, TR), bf16),
                pltpu.VMEM((256, TR), bf16),
            ],
        ),
        compiler_params=pltpu.CompilerParams(vmem_limit_bytes=VMEM_LIMIT),
        name="update",
    )(
        table, diag, y, factors,
        *[strips.reshape(2, 8, 8, BLK, BLK)] * 4,
        *[recv.reshape(2, 8, 8, BLK, BLK)] * 4,
    )


def body(child_blocks, block_map, front_diagonal):
    diag = front_diagonal.reshape(128, BLK)
    send, table = pack(block_map, child_blocks)
    recv, strips = exchange(send)
    strips = strips.reshape(16, 8, BLK, BLK)
    y, factors = pivots(table, diag, recv, strips)
    y = spread(y)
    return update(table, diag, y, factors, strips, recv)


def solution(mesh):
    return jax.shard_map(
        body,
        mesh=mesh,
        in_specs=(P("row", "col"), P(), P()),
        out_specs=P("row", "col"),
        check_vma=False,
    )
```

```python
import jax
import jax.numpy as jnp
from jax import lax
from jax.experimental import pallas as pl
from jax.experimental.pallas import tpu as pltpu
from jax.sharding import PartitionSpec as P

BLK = 128
PW = 512
TR = 1024
TC = 2048
MESH = pl.DeviceIdType.MESH
VMEM_LIMIT = 56 * 1024 * 1024
ANY = pl.BlockSpec(memory_space=pl.ANY)
SMEM = pl.BlockSpec(memory_space=pltpu.SMEM)
VMEM = pl.BlockSpec(memory_space=pltpu.VMEM)
HBM = pl.BlockSpec(memory_space=pltpu.HBM)


def pack_kernel(map_ref, child_ref, send_ref, table_ref, sem):
    row, col = lax.axis_index("row"), lax.axis_index("col")
    child, group = row // 8, row % 8

    def start(step, carry):
        t, u = step // 8, step % 8
        q = map_ref[child, group * 8 + t] // 16
        c = map_ref[child, col * 8 + u] // 16
        block = child_ref.at[
            pl.ds(pl.multiple_of(t * BLK, BLK), BLK), pl.ds(pl.multiple_of(u * BLK, BLK), BLK)
        ]
        pltpu.make_async_copy(block, send_ref.at[q * 8 + c], sem).start()
        return carry

    lax.fori_loop(0, 64, start, 0)

    def clear(step, carry):
        table_ref[step // 32, step % 32] = -1
        return carry

    lax.fori_loop(0, 64, clear, 0)

    def look(step, carry):
        k, s = step // 64, step % 64
        b = map_ref[k, s]

        @pl.when(b // 8 == row)
        def _():
            table_ref[k, b % 8] = s // 8

        @pl.when(b // 16 == col)
        def _():
            table_ref[k, 8 + b % 16] = s // 8

        @pl.when(b < 8)
        def _():
            table_ref[k, 24 + b] = s // 8

        return carry

    lax.fori_loop(0, 128, look, 0)
    pltpu.make_async_copy(send_ref, send_ref, sem).wait()


def pack(block_map, child):
    return pl.pallas_call(
        pack_kernel,
        out_shape=(
            jax.ShapeDtypeStruct((64, BLK, BLK), jnp.float32),
            jax.ShapeDtypeStruct((2, 32), jnp.int32),
        ),
        in_specs=[SMEM, VMEM],
        out_specs=(HBM, SMEM),
        scratch_shapes=[pltpu.SemaphoreType.DMA],
        compiler_params=pltpu.CompilerParams(vmem_limit_bytes=VMEM_LIMIT),
        name="pack",
    )(block_map, child)


def exchange_kernel(
    send_ref, recv_ref, strip_ref, main_s, main_r, col_s, col_r, own_sem, gat_s, gat_r
):
    row, col = lax.axis_index("row"), lax.axis_index("col")
    me = row * 8 + col
    x, y = row % 4, row // 4

    own_a = pltpu.make_async_copy(send_ref.at[(row // 2) * 8 + col], recv_ref.at[me], own_sem.at[0])
    own_b = pltpu.make_async_copy(send_ref.at[col], strip_ref.at[y, x, col], own_sem.at[1])
    own_a.start()
    own_b.start()

    def send_strip(step, carry):
        to = (col + step) % 8
        pltpu.make_async_remote_copy(
            send_ref.at[to], strip_ref.at[y, x, col], col_s, col_r,
            device_id=(row, to), device_id_type=MESH,
        ).start()
        return carry

    lax.fori_loop(1, 8, send_strip, 0)

    def send_block(step, carry):
        to = (me + step * 45) % 128
        to_row, to_col = to // 8, to % 8
        pltpu.make_async_remote_copy(
            send_ref.at[(to_row // 2) * 8 + to_col], recv_ref.at[me], main_s, main_r,
            device_id=(to_row, to_col), device_id_type=MESH,
        ).start()
        return carry

    xp, xm = y * 4 + (x + 1) % 4, y * 4 + (x + 3) % 4
    yp, ym = ((y + 1) % 4) * 4 + x, ((y + 3) % 4) * 4 + x
    xl, xr = (x + 3) % 4, (x + 1) % 4
    yl, yr = (y + 3) % 4, (y + 1) % 4

    def hop(index, piece, to_row):
        ref = strip_ref.at[piece]
        return pltpu.make_async_remote_copy(
            ref, ref, gat_s.at[index], gat_r.at[index],
            device_id=(to_row, col), device_id_type=MESH,
        )

    def landed(index, piece):
        ref = strip_ref.at[piece]
        pltpu.make_async_remote_copy(
            ref, ref, gat_s.at[index], gat_r.at[index],
            device_id=(row, col), device_id_type=MESH,
        ).wait_recv()

    lo, hi = pl.ds(0, 4), pl.ds(4, 4)
    two = [pl.ds(2 * i, 2) for i in range(4)]
    every = pl.ds(0, 4)

    seven = strip_ref.at[y, x, pl.ds(0, 7)]
    pltpu.make_async_remote_copy(
        seven, seven, col_s, col_r, device_id=(row, col), device_id_type=MESH
    ).wait()
    own_b.wait()

    hops = []

    def go(index, piece, to_row):
        copy = hop(index, piece, to_row)
        copy.start()
        hops.append(copy)

    go(0, (y, x, lo), xp)
    go(1, (y, x, lo), xm)
    go(2, (y, x, hi), yp)
    go(3, (y, x, hi), ym)
    lax.fori_loop(1, 32, send_block, 0)
    landed(0, (y, xl, lo))
    go(4, (y, xl, two[0]), xp)
    landed(1, (y, xr, lo))
    go(5, (y, xr, two[1]), xm)
    landed(2, (yl, x, hi))
    go(6, (yl, x, two[2]), yp)
    landed(3, (yr, x, hi))
    go(7, (yr, x, two[3]), ym)
    lax.fori_loop(32, 64, send_block, 0)
    xo, yo = (x + 2) % 4, (y + 2) % 4
    landed(4, (y, xo, two[0]))
    landed(5, (y, xo, two[1]))
    go(8, (y, every, lo), yp)
    go(9, (y, every, lo), ym)
    landed(6, (yo, x, two[2]))
    landed(7, (yo, x, two[3]))
    go(10, (every, x, hi), xp)
    go(11, (every, x, hi), xm)
    lax.fori_loop(64, 96, send_block, 0)
    first, last = pl.ds(0, 2), pl.ds(2, 2)
    landed(8, (yl, every, lo))
    go(12, (yl, first, lo), yp)
    landed(9, (yr, every, lo))
    go(13, (yr, last, lo), ym)
    landed(10, (every, xl, hi))
    go(14, (first, xl, hi), xp)
    landed(11, (every, xr, hi))
    go(15, (last, xr, hi), xm)
    lax.fori_loop(96, 128, send_block, 0)
    landed(12, (yo, first, lo))
    landed(13, (yo, last, lo))
    landed(14, (first, xo, hi))
    landed(15, (last, xo, hi))
    for copy in hops:
        copy.wait_send()
    own_a.wait()
    rest = recv_ref.at[pl.ds(0, 127)]
    pltpu.make_async_remote_copy(
        rest, rest, main_s, main_r, device_id=(row, col), device_id_type=MESH
    ).wait()


def exchange(send):
    dma = pltpu.SemaphoreType.DMA
    return pl.pallas_call(
        exchange_kernel,
        out_shape=(
            jax.ShapeDtypeStruct((128, BLK, BLK), jnp.float32),
            jax.ShapeDtypeStruct((4, 4, 8, BLK, BLK), jnp.float32),
        ),
        in_specs=[ANY],
        out_specs=(HBM, HBM),
        scratch_shapes=[dma, dma, dma, dma, dma((2,)), dma((16,)), dma((16,))],
        compiler_params=pltpu.CompilerParams(has_side_effects=True),
        name="exchange",
    )(send)


def split(value):
    high = value.astype(jnp.bfloat16)
    return high, (value - high.astype(jnp.float32)).astype(jnp.bfloat16)


def dot1(a, b):
    return jnp.dot(a, b, preferred_element_type=jnp.float32)


def dot3(a, b):
    return dot1(a[0], b[0]) + (dot1(a[0], b[1]) + dot1(a[1], b[0]))


def identity(n):
    return lax.broadcasted_iota(jnp.int32, (n, n), 0) == lax.broadcasted_iota(jnp.int32, (n, n), 1)


def inverse_into(matrix_ref, scaled_ref, x_ref, out_ref):
    eye = identity(PW)
    matrix = matrix_ref[...]
    diagonal = jnp.where(eye, matrix, 0.0)
    by_col = lax.rsqrt(jnp.sum(diagonal, axis=0, keepdims=True))
    by_row = lax.rsqrt(jnp.sum(diagonal, axis=1, keepdims=True))
    scaled = matrix * by_row * by_col
    scaled_ref[...] = scaled
    bound = jnp.max(jnp.sum(jnp.abs(scaled), axis=0, keepdims=True))
    alpha = jnp.minimum(1.0, 1.9 / bound)

    def begin():
        x_ref[...] = jnp.where(eye, 2.0 * alpha, 0.0) - alpha * alpha * scaled_ref[...]

    def run(most, settled, first, second):
        def step(carry):
            count, _ = carry
            value = x_ref[...]
            residual = jnp.where(eye, 1.0, 0.0) - first(scaled_ref[...], value)
            x_ref[...] += second(value, residual)
            return count + 1, jnp.sum(residual * residual)

        return lax.while_loop(
            lambda carry: (carry[0] < most) & (carry[1] > settled), step, (jnp.int32(0), jnp.float32(1e9))
        )[1]

    def once(a, b):
        return dot1(a.astype(jnp.bfloat16), b.astype(jnp.bfloat16))

    def thrice(a, b):
        return dot3(split(a), split(b))

    begin()
    run(10, 1.0, once, once)
    left = run(5, 1e-6, thrice, once)

    @pl.when(jnp.logical_not(left <= 1e-6))
    def _():
        begin()
        run(48, 1e-6, thrice, thrice)

    residual = jnp.where(eye, 1.0, 0.0) - jnp.dot(
        scaled_ref[...], x_ref[...], precision=lax.Precision.HIGHEST, preferred_element_type=jnp.float32
    )
    value = x_ref[...]
    value = value + thrice(value, residual)
    out_ref[...] = value * by_row * by_col


def pivot_kernel(
    table_ref, diag_ref, recv_ref, strip_ref, y_ref, f_ref,
    strips, blocks, piv, tile, inv0, inv1, l10, scaled, newton, schur, sems,
):
    row, col = lax.axis_index("row"), lax.axis_index("col")

    @pl.when(col == 0)
    def _():
        load_a = pltpu.make_async_copy(strip_ref, strips, sems.at[0])
        load_b = pltpu.make_async_copy(recv_ref, blocks, sems.at[1])
        load_a.start()
        load_b.start()
        load_a.wait()

        def pivot_block(step, carry):
            a, b = step // 8, step % 8
            total = jnp.where(identity(BLK) & (a == b), diag_ref[pl.ds(a, 1), :], 0.0)
            for k in range(2):
                ga, gb = table_ref[k, 24 + a], table_ref[k, 24 + b]
                value = strips[k * 8 + jnp.maximum(ga, 0), jnp.maximum(gb, 0)]
                total = total + jnp.where((ga >= 0) & (gb >= 0), value, 0.0)
            piv[pl.ds(pl.multiple_of(a * BLK, BLK), BLK), pl.ds(pl.multiple_of(b * BLK, BLK), BLK)] = total
            return carry

        lax.fori_loop(0, 64, pivot_block, 0)
        schur[...] = piv[:PW, :PW]
        inverse_into(schur, scaled, newton, inv0)
        l10[...] = dot3(split(piv[PW:, :PW]), split(inv0[...]))
        schur[...] = piv[PW:, PW:] - dot3(split(l10[...]), split(piv[:PW, PW:]))

        load_b.wait()

        @pl.when(row == 0)
        def _():
            f_ref[:PW, :] = piv[:PW, :]
            f_ref[PW:, :PW] = l10[...]
            f_ref[PW:, PW:] = schur[...]
            y_ref[...] = jnp.zeros((TR, TR), jnp.float32)
            y_ref[PW:, :PW] = l10[...]

        @pl.when(row > 0)
        def _():
            inverse_into(schur, scaled, newton, inv1)

            def tile_block(step, carry):
                a, b = step // 8, step % 8
                total = jnp.zeros((BLK, BLK), jnp.float32)
                for k in range(2):
                    ga, hb = table_ref[k, a], table_ref[k, 24 + b]
                    value = blocks[k * 64 + jnp.maximum(ga, 0) * 8 + jnp.maximum(hb, 0)]
                    total = total + jnp.where((ga >= 0) & (hb >= 0), value, 0.0)
                tile[pl.ds(pl.multiple_of(a * BLK, BLK), BLK), pl.ds(pl.multiple_of(b * BLK, BLK), BLK)] = total
                return carry

            lax.fori_loop(0, 64, tile_block, 0)
            for part in range(2):
                rows = pl.ds(part * PW, PW)
                factor0 = dot3(split(tile[rows, :PW]), split(inv0[...]))
                f_ref[rows, :PW] = factor0
                rest = tile[rows, PW:] - dot3(split(factor0), split(piv[:PW, PW:]))
                factor1 = dot3(split(rest), split(inv1[...]))
                f_ref[rows, PW:] = factor1
                y_ref[rows, PW:] = factor1
                y_ref[rows, :PW] = f_ref[rows, :PW] - dot3(split(factor1), split(l10[...]))


def pivots(table, diag, recv, strips):
    f32 = jnp.float32
    half = pltpu.VMEM((PW, PW), f32)
    return pl.pallas_call(
        pivot_kernel,
        out_shape=(jax.ShapeDtypeStruct((TR, TR), f32), jax.ShapeDtypeStruct((TR, TR), f32)),
        in_specs=[SMEM, VMEM, ANY, ANY],
        out_specs=(VMEM, VMEM),
        scratch_shapes=[
            pltpu.VMEM((16, 8, BLK, BLK), f32),
            pltpu.VMEM((128, BLK, BLK), f32),
            pltpu.VMEM((TR, TR), f32),
            pltpu.VMEM((TR, TR), f32),
            half, half, half, half, half, half,
            pltpu.SemaphoreType.DMA((2,)),
        ],
        compiler_params=pltpu.CompilerParams(vmem_limit_bytes=VMEM_LIMIT),
        name="pivots",
    )(table, diag, recv, strips)


CHUNKS = 16


def spread_kernel(y_ref, out_ref, ring_s, ring_r, core_s, core_r):
    row, col = lax.axis_index("row"), lax.axis_index("col")
    z, core = col // 2, col % 2
    size = TR // CHUNKS

    def ring(source, t):
        step = 1 if t % 2 == 0 else 3
        rows = pl.ds(t * size, size)
        return pltpu.make_async_remote_copy(
            source.at[rows], out_ref.at[rows], ring_s.at[t], ring_r.at[t],
            device_id=(row, ((z + step) % 4) * 2), device_id_type=MESH,
        )

    def across(source, t):
        rows = pl.ds(t * size, size)
        return pltpu.make_async_remote_copy(
            source.at[rows], out_ref.at[rows], core_s.at[t], core_r.at[t],
            device_id=(row, z * 2 + 1), device_id_type=MESH,
        )

    @pl.when(col == 0)
    def _():
        for t in range(CHUNKS):
            if t >= 4:
                ring(y_ref, t - 4).wait_send()
            ring(y_ref, t).start()
            across(y_ref, t).start()
        for t in range(CHUNKS):
            if t >= CHUNKS - 4:
                ring(y_ref, t).wait_send()
            across(y_ref, t).wait_send()

    def relay(place):
        def due(t):
            return t // 2 + (place if t % 2 == 0 else 4 - place)

        for t in sorted(range(CHUNKS), key=lambda t: (due(t), t)):
            ring(out_ref, t).wait_recv()
            if place != (3 if t % 2 == 0 else 1):
                ring(out_ref, t).start()
            across(out_ref, t).start()
        for t in range(CHUNKS):
            if place != (3 if t % 2 == 0 else 1):
                ring(out_ref, t).wait_send()
            across(out_ref, t).wait_send()

    for place in range(1, 4):

        @pl.when((core == 0) & (z == place))
        def _(place=place):
            relay(place)

    @pl.when(core == 1)
    def _():
        for t in range(CHUNKS):
            across(out_ref, t).wait_recv()


def spread(y):
    dma = pltpu.SemaphoreType.DMA
    return pl.pallas_call(
        spread_kernel,
        out_shape=jax.ShapeDtypeStruct((TR, TR), jnp.float32),
        in_specs=[HBM],
        out_specs=HBM,
        scratch_shapes=[dma((CHUNKS,)), dma((CHUNKS,)), dma((CHUNKS,)), dma((CHUNKS,))],
        compiler_params=pltpu.CompilerParams(has_side_effects=True),
        name="spread",
    )(y)


def update_kernel(table_ref, diag_ref, f_ref, own_ref, came_ref, *refs):
    strips, blocks = refs[0:4], refs[4:8]
    out_ref, y, yh, yl, uh, ul, sem = refs[8:]
    row, col = lax.axis_index("row"), lax.axis_index("col")
    step = pl.program_id(0)

    @pl.when(step == 0)
    def _():
        @pl.when(col == 0)
        def _():
            copy = pltpu.make_async_copy(own_ref, y, sem)
            copy.start()
            copy.wait()

        @pl.when(col != 0)
        def _():
            copy = pltpu.make_async_copy(came_ref, y, sem)
            copy.start()
            copy.wait()

        yh[...], yl[...] = split(y[...])

    factors = (col == 0) & (step < 4)

    @pl.when(factors)
    def _():
        out_ref[...] = f_ref[...]

    @pl.when(jnp.logical_not(factors))
    def _():
        for u in range(2):
            j = step * 2 + u

            def strip_block(i, carry):
                on = identity(BLK) & (col * 16 + j == i)
                total = jnp.where(on, diag_ref[pl.ds(i, 1), :], 0.0)
                for k in range(2):
                    g, h = table_ref[k, 24 + i], table_ref[k, 8 + j]
                    value = strips[2 * u + k][0, jnp.maximum(g, 0), 0]
                    total = total + jnp.where((g >= 0) & (h >= 0), value, 0.0)
                at = pl.ds(pl.multiple_of(i * BLK, BLK), BLK)
                uh[at, pl.ds(u * BLK, BLK)], ul[at, pl.ds(u * BLK, BLK)] = split(total)
                return carry

            lax.fori_loop(0, 8, strip_block, 0)

        out_ref[...] = dot3((yh[...], yl[...]), (uh[...], ul[...]))
        for u in range(2):
            j = step * 2 + u

            def front_block(i, carry):
                on = identity(BLK) & (col * 16 + j == row * 8 + i)
                total = jnp.where(on, diag_ref[pl.ds(row * 8 + i, 1), :], 0.0)
                for k in range(2):
                    g, h = table_ref[k, i], table_ref[k, 8 + j]
                    value = blocks[2 * u + k][0, jnp.maximum(g, 0), 0]
                    total = total + jnp.where((g >= 0) & (h >= 0), value, 0.0)
                at = pl.ds(pl.multiple_of(i * BLK, BLK), BLK), pl.ds(u * BLK, BLK)
                out_ref[at] = total - out_ref[at]
                return carry

            lax.fori_loop(0, 8, front_block, 0)


def update(table, diag, factors, own, came, strips, recv):
    f32, bf16 = jnp.float32, jnp.bfloat16

    def spec(u, k):
        return pl.BlockSpec(
            (1, 8, 1, BLK, BLK),
            lambda s, table: (k, 0, jnp.maximum(table[k, 8 + 2 * s + u], 0), 0, 0),
        )

    column_specs = [spec(u, k) for u in range(2) for k in range(2)]
    return pl.pallas_call(
        update_kernel,
        out_shape=jax.ShapeDtypeStruct((TR, TC), f32),
        grid_spec=pltpu.PrefetchScalarGridSpec(
            num_scalar_prefetch=1,
            grid=(8,),
            in_specs=[
                pl.BlockSpec((128, BLK), lambda s, table: (0, 0)),
                pl.BlockSpec((TR, 256), lambda s, table: (0, jnp.minimum(s, 3))),
                HBM,
                HBM,
                *column_specs,
                *column_specs,
            ],
            out_specs=pl.BlockSpec((TR, 256), lambda s, table: (0, s)),
            scratch_shapes=[
                pltpu.VMEM((TR, TR), f32),
                pltpu.VMEM((TR, TR), bf16),
                pltpu.VMEM((TR, TR), bf16),
                pltpu.VMEM((TR, 256), bf16),
                pltpu.VMEM((TR, 256), bf16),
                pltpu.SemaphoreType.DMA,
            ],
        ),
        compiler_params=pltpu.CompilerParams(vmem_limit_bytes=VMEM_LIMIT),
        name="update",
    )(
        table, diag, factors, own, came,
        *[strips.reshape(2, 8, 8, BLK, BLK)] * 4,
        *[recv.reshape(2, 8, 8, BLK, BLK)] * 4,
    )


def body(child_blocks, block_map, front_diagonal):
    diag = front_diagonal.reshape(128, BLK)
    send, table = pack(block_map, child_blocks)
    recv, strips = exchange(send)
    strips = strips.reshape(16, 8, BLK, BLK)
    y, factors = pivots(table, diag, recv, strips)
    came = spread(y)
    return update(table, diag, factors, y, came, strips, recv)


def solution(mesh):
    return jax.shard_map(
        body,
        mesh=mesh,
        in_specs=(P("row", "col"), P(), P()),
        out_specs=P("row", "col"),
        check_vma=False,
    )
```

```python
import jax
import jax.numpy as jnp
from jax import lax
from jax.experimental import pallas as pl
from jax.experimental.pallas import tpu as pltpu
from jax.sharding import PartitionSpec as P

BLK = 128
PW = 512
TOP = 80
BOT = BLK - TOP
TR = 1024
TC = 2048
MESH = pl.DeviceIdType.MESH
VMEM_LIMIT = 56 * 1024 * 1024
ANY = pl.BlockSpec(memory_space=pl.ANY)
SMEM = pl.BlockSpec(memory_space=pltpu.SMEM)
VMEM = pl.BlockSpec(memory_space=pltpu.VMEM)
HBM = pl.BlockSpec(memory_space=pltpu.HBM)


def pack_kernel(map_ref, child_ref, send_ref, rest_ref, table_ref, sem, rest_sem):
    row, col = lax.axis_index("row"), lax.axis_index("col")
    child, group = row // 8, row % 8

    def start(step, carry):
        t, u = step // 8, step % 8
        q = map_ref[child, group * 8 + t] // 16
        c = map_ref[child, col * 8 + u] // 16
        block = child_ref.at[
            pl.ds(pl.multiple_of(t * BLK, BLK), BLK), pl.ds(pl.multiple_of(u * BLK, BLK), BLK)
        ]
        pltpu.make_async_copy(block, send_ref.at[q * 8 + c], sem).start()
        rest = child_ref.at[
            pl.ds(pl.multiple_of(t * BLK + TOP, 16), BOT), pl.ds(pl.multiple_of(u * BLK, BLK), BLK)
        ]
        pltpu.make_async_copy(rest, rest_ref.at[q * 16 + c], rest_sem).start()
        pltpu.make_async_copy(rest, rest_ref.at[q * 16 + 8 + c], rest_sem).start()
        return carry

    lax.fori_loop(0, 64, start, 0)

    def clear(step, carry):
        table_ref[step // 32, step % 32] = -1
        return carry

    lax.fori_loop(0, 64, clear, 0)

    def look(step, carry):
        k, s = step // 64, step % 64
        b = map_ref[k, s]

        @pl.when(b // 8 == row)
        def _():
            table_ref[k, b % 8] = s // 8

        @pl.when(b // 16 == col)
        def _():
            table_ref[k, 8 + b % 16] = s // 8

        @pl.when(b < 8)
        def _():
            table_ref[k, 24 + b] = s // 8

        return carry

    lax.fori_loop(0, 128, look, 0)
    for k in range(2):
        for j in range(16):
            here = table_ref[k, 8 + j]
            before = table_ref[k, 32 + j - 2] if j >= 2 else 0
            table_ref[k, 32 + j] = jnp.where(here >= 0, here, before)
    pltpu.make_async_copy(send_ref, send_ref, sem).wait()
    pltpu.make_async_copy(rest_ref, rest_ref, rest_sem).wait()


def pack(block_map, child):
    return pl.pallas_call(
        pack_kernel,
        out_shape=(
            jax.ShapeDtypeStruct((64, BLK, BLK), jnp.float32),
            jax.ShapeDtypeStruct((128, BOT, BLK), jnp.float32),
            jax.ShapeDtypeStruct((2, 48), jnp.int32),
        ),
        in_specs=[SMEM, VMEM],
        out_specs=(HBM, HBM, SMEM),
        scratch_shapes=[pltpu.SemaphoreType.DMA, pltpu.SemaphoreType.DMA],
        compiler_params=pltpu.CompilerParams(vmem_limit_bytes=VMEM_LIMIT),
        name="pack",
    )(block_map, child)


def exchange_kernel(
    send_ref, recv_ref, left_ref, strip_ref,
    main_s, main_r, left_s, left_r, col_s, col_r, own_sem, gat_s, gat_r,
):
    row, col = lax.axis_index("row"), lax.axis_index("col")
    me = row * 8 + col
    x, y = row % 4, row // 4

    top, bottom = pl.ds(0, TOP), pl.ds(TOP, BOT)
    own = send_ref.at[(row // 2) * 8]
    own_a = pltpu.make_async_copy(own.at[top], recv_ref.at[me], own_sem.at[0])
    own_c = pltpu.make_async_copy(own.at[bottom], left_ref.at[me], own_sem.at[2])
    own_b = pltpu.make_async_copy(send_ref.at[col], strip_ref.at[y, x, col], own_sem.at[1])

    @pl.when(col == 0)
    def _():
        own_a.start()
        own_c.start()

    own_b.start()

    def send_strip(step, carry):
        to = (col + step) % 8
        pltpu.make_async_remote_copy(
            send_ref.at[to], strip_ref.at[y, x, col], col_s, col_r,
            device_id=(row, to), device_id_type=MESH,
        ).start()
        return carry

    lax.fori_loop(1, 8, send_strip, 0)

    def send_block(step, carry):
        to = (me + step * 45) % 128
        to_row, to_col = to // 8, to % 8
        block = send_ref.at[(to_row // 2) * 8 + to_col]

        @pl.when((to_col == 0) | (to_col // 2 != col // 2))
        def _():
            pltpu.make_async_remote_copy(
                block.at[top], recv_ref.at[me], main_s, main_r,
                device_id=(to_row, to_col), device_id_type=MESH,
            ).start()

        @pl.when(to_col == 0)
        def _():
            pltpu.make_async_remote_copy(
                block.at[bottom], left_ref.at[me], left_s, left_r,
                device_id=(to_row, to_col), device_id_type=MESH,
            ).start()

        return carry

    xp, xm = y * 4 + (x + 1) % 4, y * 4 + (x + 3) % 4
    yp, ym = ((y + 1) % 4) * 4 + x, ((y + 3) % 4) * 4 + x
    xl, xr = (x + 3) % 4, (x + 1) % 4
    yl, yr = (y + 3) % 4, (y + 1) % 4

    def hop(index, piece, to_row):
        ref = strip_ref.at[piece]
        return pltpu.make_async_remote_copy(
            ref, ref, gat_s.at[index], gat_r.at[index],
            device_id=(to_row, col), device_id_type=MESH,
        )

    def landed(index, piece):
        ref = strip_ref.at[piece]
        pltpu.make_async_remote_copy(
            ref, ref, gat_s.at[index], gat_r.at[index],
            device_id=(row, col), device_id_type=MESH,
        ).wait_recv()

    lo, hi = pl.ds(0, 4), pl.ds(4, 4)
    two = [pl.ds(2 * i, 2) for i in range(4)]
    every = pl.ds(0, 4)

    seven = strip_ref.at[y, x, pl.ds(0, 7)]
    pltpu.make_async_remote_copy(
        seven, seven, col_s, col_r, device_id=(row, col), device_id_type=MESH
    ).wait()
    own_b.wait()

    hops = []

    def go(index, piece, to_row):
        copy = hop(index, piece, to_row)
        copy.start()
        hops.append(copy)

    go(0, (y, x, lo), xp)
    go(1, (y, x, lo), xm)
    go(2, (y, x, hi), yp)
    go(3, (y, x, hi), ym)
    lax.fori_loop(1, 32, send_block, 0)
    landed(0, (y, xl, lo))
    go(4, (y, xl, two[0]), xp)
    landed(1, (y, xr, lo))
    go(5, (y, xr, two[1]), xm)
    landed(2, (yl, x, hi))
    go(6, (yl, x, two[2]), yp)
    landed(3, (yr, x, hi))
    go(7, (yr, x, two[3]), ym)
    lax.fori_loop(32, 64, send_block, 0)
    xo, yo = (x + 2) % 4, (y + 2) % 4
    landed(4, (y, xo, two[0]))
    landed(5, (y, xo, two[1]))
    go(8, (y, every, lo), yp)
    go(9, (y, every, lo), ym)
    landed(6, (yo, x, two[2]))
    landed(7, (yo, x, two[3]))
    go(10, (every, x, hi), xp)
    go(11, (every, x, hi), xm)
    lax.fori_loop(64, 96, send_block, 0)
    first, last = pl.ds(0, 2), pl.ds(2, 2)
    landed(8, (yl, every, lo))
    go(12, (yl, first, lo), yp)
    landed(9, (yr, every, lo))
    go(13, (yr, last, lo), ym)
    landed(10, (every, xl, hi))
    go(14, (first, xl, hi), xp)
    landed(11, (every, xr, hi))
    go(15, (last, xr, hi), xm)
    lax.fori_loop(96, 128, send_block, 0)
    landed(12, (yo, first, lo))
    landed(13, (yo, last, lo))
    landed(14, (first, xo, hi))
    landed(15, (last, xo, hi))
    for copy in hops:
        copy.wait_send()

    def blocks(ref, count, send_sem, recv_sem):
        part = ref.at[pl.ds(0, count)]
        return pltpu.make_async_remote_copy(
            part, part, send_sem, recv_sem, device_id=(row, col), device_id_type=MESH
        )

    @pl.when(col == 0)
    def _():
        own_a.wait()
        own_c.wait()
        blocks(recv_ref, 111, main_s, main_r).wait_send()
        blocks(left_ref, 15, left_s, left_r).wait_send()
        blocks(recv_ref, 127, main_s, main_r).wait_recv()
        blocks(left_ref, 127, left_s, left_r).wait_recv()

    @pl.when(col == 1)
    def _():
        blocks(recv_ref, 112, main_s, main_r).wait_send()

    @pl.when(col > 1)
    def _():
        blocks(recv_ref, 96, main_s, main_r).wait_send()

    @pl.when(col > 0)
    def _():
        blocks(left_ref, 16, left_s, left_r).wait_send()
        blocks(recv_ref, 96, main_s, main_r).wait_recv()


def exchange(send):
    dma = pltpu.SemaphoreType.DMA
    return pl.pallas_call(
        exchange_kernel,
        out_shape=(
            jax.ShapeDtypeStruct((128, TOP, BLK), jnp.float32),
            jax.ShapeDtypeStruct((128, BOT, BLK), jnp.float32),
            jax.ShapeDtypeStruct((4, 4, 8, BLK, BLK), jnp.float32),
        ),
        in_specs=[HBM],
        out_specs=(HBM, HBM, HBM),
        scratch_shapes=[dma, dma, dma, dma, dma, dma, dma((3,)), dma((16,)), dma((16,))],
        compiler_params=pltpu.CompilerParams(has_side_effects=True, vmem_limit_bytes=VMEM_LIMIT),
        name="exchange",
    )(send)


def split(value):
    high = value.astype(jnp.bfloat16)
    return high, (value - high.astype(jnp.float32)).astype(jnp.bfloat16)


def dot1(a, b):
    return jnp.dot(a, b, preferred_element_type=jnp.float32)


def dot3(a, b):
    return dot1(a[0], b[0]) + (dot1(a[0], b[1]) + dot1(a[1], b[0]))


def identity(n):
    return lax.broadcasted_iota(jnp.int32, (n, n), 0) == lax.broadcasted_iota(jnp.int32, (n, n), 1)


def inverse_into(matrix_ref, scaled_ref, x_ref, out_ref):
    eye = identity(PW)
    matrix = matrix_ref[...]
    diagonal = jnp.where(eye, matrix, 0.0)
    by_col = lax.rsqrt(jnp.sum(diagonal, axis=0, keepdims=True))
    by_row = lax.rsqrt(jnp.sum(diagonal, axis=1, keepdims=True))
    scaled = matrix * by_row * by_col
    scaled_ref[...] = scaled
    bound = jnp.max(jnp.sum(jnp.abs(scaled), axis=0, keepdims=True))
    alpha = jnp.minimum(1.0, 1.9 / bound)

    def begin():
        x_ref[...] = jnp.where(eye, 2.0 * alpha, 0.0) - alpha * alpha * scaled_ref[...]

    def run(most, settled, first, second):
        def step(carry):
            count, _ = carry
            value = x_ref[...]
            residual = jnp.where(eye, 1.0, 0.0) - first(scaled_ref[...], value)
            x_ref[...] += second(value, residual)
            return count + 1, jnp.sum(residual * residual)

        return lax.while_loop(
            lambda carry: (carry[0] < most) & (carry[1] > settled), step, (jnp.int32(0), jnp.float32(1e9))
        )[1]

    def once(a, b):
        return dot1(a.astype(jnp.bfloat16), b.astype(jnp.bfloat16))

    def thrice(a, b):
        return dot3(split(a), split(b))

    begin()
    run(10, 1.0, once, once)
    left = run(5, 1e-6, thrice, once)

    @pl.when(jnp.logical_not(left <= 1e-6))
    def _():
        begin()
        run(48, 1e-6, thrice, thrice)

    residual = jnp.where(eye, 1.0, 0.0) - jnp.dot(
        scaled_ref[...], x_ref[...], precision=lax.Precision.HIGHEST, preferred_element_type=jnp.float32
    )
    value = x_ref[...]
    value = value + thrice(value, residual)
    out_ref[...] = value * by_row * by_col


def pivot_kernel(
    table_ref, diag_ref, recv_ref, left_ref, strip_ref, y_ref, f_ref,
    strips, blocks, piv, tile, inv0, inv1, l10, scaled, newton, schur, sems,
):
    row, col = lax.axis_index("row"), lax.axis_index("col")

    @pl.when(col == 0)
    def _():
        load_a = pltpu.make_async_copy(strip_ref, strips, sems.at[0])
        load_b = pltpu.make_async_copy(recv_ref, blocks.at[:, pl.ds(0, TOP)], sems.at[1])
        load_c = pltpu.make_async_copy(left_ref, blocks.at[:, pl.ds(TOP, BOT)], sems.at[2])
        load_a.start()
        load_b.start()
        load_c.start()
        load_a.wait()

        def pivot_block(step, carry):
            a, b = step // 8, step % 8
            total = jnp.where(identity(BLK) & (a == b), diag_ref[pl.ds(a, 1), :], 0.0)
            for k in range(2):
                ga, gb = table_ref[k, 24 + a], table_ref[k, 24 + b]
                value = strips[k * 8 + jnp.maximum(ga, 0), jnp.maximum(gb, 0)]
                total = total + jnp.where((ga >= 0) & (gb >= 0), value, 0.0)
            piv[pl.ds(pl.multiple_of(a * BLK, BLK), BLK), pl.ds(pl.multiple_of(b * BLK, BLK), BLK)] = total
            return carry

        lax.fori_loop(0, 64, pivot_block, 0)
        schur[...] = piv[:PW, :PW]
        inverse_into(schur, scaled, newton, inv0)
        l10[...] = dot3(split(piv[PW:, :PW]), split(inv0[...]))
        schur[...] = piv[PW:, PW:] - dot3(split(l10[...]), split(piv[:PW, PW:]))

        load_b.wait()
        load_c.wait()

        @pl.when(row == 0)
        def _():
            f_ref[:PW, :] = piv[:PW, :]
            f_ref[PW:, :PW] = l10[...]
            f_ref[PW:, PW:] = schur[...]
            y_ref[...] = jnp.zeros((TR, TR), jnp.float32)
            y_ref[PW:, :PW] = l10[...]

        @pl.when(row > 0)
        def _():
            inverse_into(schur, scaled, newton, inv1)

            def tile_block(step, carry):
                a, b = step // 8, step % 8
                total = jnp.zeros((BLK, BLK), jnp.float32)
                for k in range(2):
                    ga, hb = table_ref[k, a], table_ref[k, 24 + b]
                    value = blocks[k * 64 + jnp.maximum(ga, 0) * 8 + jnp.maximum(hb, 0)]
                    total = total + jnp.where((ga >= 0) & (hb >= 0), value, 0.0)
                tile[pl.ds(pl.multiple_of(a * BLK, BLK), BLK), pl.ds(pl.multiple_of(b * BLK, BLK), BLK)] = total
                return carry

            lax.fori_loop(0, 64, tile_block, 0)
            for part in range(2):
                rows = pl.ds(part * PW, PW)
                factor0 = dot3(split(tile[rows, :PW]), split(inv0[...]))
                f_ref[rows, :PW] = factor0
                rest = tile[rows, PW:] - dot3(split(factor0), split(piv[:PW, PW:]))
                factor1 = dot3(split(rest), split(inv1[...]))
                f_ref[rows, PW:] = factor1
                y_ref[rows, PW:] = factor1
                y_ref[rows, :PW] = f_ref[rows, :PW] - dot3(split(factor1), split(l10[...]))


def pivots(table, diag, recv, left, strips):
    f32 = jnp.float32
    half = pltpu.VMEM((PW, PW), f32)
    return pl.pallas_call(
        pivot_kernel,
        out_shape=(jax.ShapeDtypeStruct((TR, TR), f32), jax.ShapeDtypeStruct((TR, TR), f32)),
        in_specs=[SMEM, VMEM, HBM, HBM, HBM],
        out_specs=(VMEM, VMEM),
        scratch_shapes=[
            pltpu.VMEM((16, 8, BLK, BLK), f32),
            pltpu.VMEM((128, BLK, BLK), f32),
            pltpu.VMEM((TR, TR), f32),
            pltpu.VMEM((TR, TR), f32),
            half, half, half, half, half, half,
            pltpu.SemaphoreType.DMA((3,)),
        ],
        compiler_params=pltpu.CompilerParams(vmem_limit_bytes=VMEM_LIMIT),
        name="pivots",
    )(table, diag, recv, left, strips)


CHUNKS = 16


def spread_kernel(
    y_ref, send_ref, _, out_ref, recv_ref, ring_s, ring_r, core_s, core_r, flat_s, flat_r, own_sem
):
    row, col = lax.axis_index("row"), lax.axis_index("col")
    me = row * 8 + col
    z, core = col // 2, col % 2
    size = TR // CHUNKS

    def ring(source, t):
        step = 1 if t % 2 == 0 else 3
        rows = pl.ds(t * size, size)
        return pltpu.make_async_remote_copy(
            source.at[rows], out_ref.at[rows], ring_s.at[t], ring_r.at[t],
            device_id=(row, ((z + step) % 4) * 2), device_id_type=MESH,
        )

    def across(source, t):
        rows = pl.ds(t * size, size)
        return pltpu.make_async_remote_copy(
            source.at[rows], out_ref.at[rows], core_s.at[t], core_r.at[t],
            device_id=(row, z * 2 + 1), device_id_type=MESH,
        )

    def flat(step, carry):
        to = (row * 2 + core + step * 11) % 32
        to_row, to_col = to // 2, z * 2 + to % 2

        @pl.when(to_col != 0)
        def _():
            pltpu.make_async_remote_copy(
                send_ref.at[(to_row // 2) * 8 + to_col, pl.ds(0, TOP)], recv_ref.at[me], flat_s, flat_r,
                device_id=(to_row, to_col), device_id_type=MESH,
            ).start()

        return carry

    def flats(count):
        part = recv_ref.at[pl.ds(0, count)]
        return pltpu.make_async_remote_copy(
            part, part, flat_s, flat_r, device_id=(row, col), device_id_type=MESH
        )

    own = pltpu.make_async_copy(
        send_ref.at[(row // 2) * 8 + col, pl.ds(0, TOP)], recv_ref.at[me], own_sem
    )

    @pl.when(col != 0)
    def _():
        own.start()

    @pl.when(col == 0)
    def _():
        for t in range(CHUNKS):
            if t >= 4:
                ring(y_ref, t - 4).wait_send()
            ring(y_ref, t).start()
            across(y_ref, t).start()
            lax.fori_loop(max(2 * t, 1), 2 * t + 2, flat, 0)
        for t in range(CHUNKS):
            if t >= CHUNKS - 4:
                ring(y_ref, t).wait_send()
            across(y_ref, t).wait_send()

    def relay(place):
        def goes(t):
            return place != (3 if t % 2 == 0 else 1)

        order = sorted(range(CHUNKS), key=lambda t: (not goes(t), t))
        for n, t in enumerate(order):
            ring(out_ref, t).wait_recv()
            if goes(t):
                ring(out_ref, t).start()
            across(out_ref, t).start()
            lax.fori_loop(max(2 * n, 1), 2 * n + 2, flat, 0)
        for t in range(CHUNKS):
            if goes(t):
                ring(out_ref, t).wait_send()
            across(out_ref, t).wait_send()

    for place in range(1, 4):

        @pl.when((core == 0) & (z == place))
        def _(place=place):
            relay(place)

    @pl.when(core == 1)
    def _():
        lax.fori_loop(1, 32, flat, 0)
        for t in range(CHUNKS):
            across(out_ref, t).wait_recv()

    @pl.when(col == 0)
    def _():
        flats(16).wait_send()

    @pl.when(col == 1)
    def _():
        flats(15).wait_send()

    @pl.when(col > 1)
    def _():
        flats(31).wait_send()

    @pl.when(col != 0)
    def _():
        flats(31).wait_recv()
        own.wait()


def spread(y, send, recv):
    dma = pltpu.SemaphoreType.DMA
    return pl.pallas_call(
        spread_kernel,
        out_shape=(
            jax.ShapeDtypeStruct((TR, TR), jnp.float32),
            jax.ShapeDtypeStruct((128, TOP, BLK), jnp.float32),
        ),
        in_specs=[HBM, HBM, HBM],
        out_specs=(HBM, HBM),
        input_output_aliases={2: 1},
        scratch_shapes=[
            dma((CHUNKS,)), dma((CHUNKS,)), dma((CHUNKS,)), dma((CHUNKS,)), dma, dma, dma,
        ],
        compiler_params=pltpu.CompilerParams(has_side_effects=True, vmem_limit_bytes=VMEM_LIMIT),
        name="spread",
    )(y, send, recv)


def update_kernel(table_ref, diag_ref, f_ref, own_ref, came_ref, *refs):
    strips, tops, bottoms = refs[0:4], refs[4:8], refs[8:12]
    out_ref, y, yh, yl, uh, ul, sem = refs[12:]
    row, col = lax.axis_index("row"), lax.axis_index("col")
    step = pl.program_id(0)

    @pl.when(step == 0)
    def _():
        @pl.when(col == 0)
        def _():
            copy = pltpu.make_async_copy(own_ref, y, sem)
            copy.start()
            copy.wait()

        @pl.when(col != 0)
        def _():
            copy = pltpu.make_async_copy(came_ref, y, sem)
            copy.start()
            copy.wait()

        yh[...], yl[...] = split(y[...])

    factors = (col == 0) & (step < 4)

    @pl.when(factors)
    def _():
        out_ref[...] = f_ref[...]

    @pl.when(jnp.logical_not(factors))
    def _():
        for u in range(2):
            j = step * 2 + u

            def strip_block(i, carry):
                on = identity(BLK) & (col * 16 + j == i)
                total = jnp.where(on, diag_ref[pl.ds(i, 1), :], 0.0)
                for k in range(2):
                    g, h = table_ref[k, 24 + i], table_ref[k, 8 + j]
                    value = strips[2 * u + k][0, jnp.maximum(g, 0), 0]
                    total = total + jnp.where((g >= 0) & (h >= 0), value, 0.0)
                at = pl.ds(pl.multiple_of(i * BLK, BLK), BLK)
                uh[at, pl.ds(u * BLK, BLK)], ul[at, pl.ds(u * BLK, BLK)] = split(total)
                return carry

            lax.fori_loop(0, 8, strip_block, 0)

        out_ref[...] = dot3((yh[...], yl[...]), (uh[...], ul[...]))
        for u in range(2):
            j = step * 2 + u

            def front_block(i, carry):
                for refs, first, count in ((tops, 0, TOP), (bottoms, TOP, BOT)):
                    there = lax.broadcasted_iota(jnp.int32, (count, BLK), 0) + first
                    on = (there == lax.broadcasted_iota(jnp.int32, (count, BLK), 1)) & (
                        col * 16 + j == row * 8 + i
                    )
                    total = jnp.where(on, diag_ref[pl.ds(row * 8 + i, 1), :], 0.0)
                    for k in range(2):
                        g, h = table_ref[k, i], table_ref[k, 8 + j]
                        value = refs[2 * u + k][0, jnp.maximum(g, 0), 0]
                        total = total + jnp.where((g >= 0) & (h >= 0), value, 0.0)
                    at = pl.ds(pl.multiple_of(i * BLK + first, 16), count), pl.ds(u * BLK, BLK)
                    out_ref[at] = total - out_ref[at]
                return carry

            lax.fori_loop(0, 8, front_block, 0)


def update(table, diag, factors, own, came, strips, recv, rest):
    f32, bf16 = jnp.float32, jnp.bfloat16

    def specs(rows):
        def spec(u, k):
            return pl.BlockSpec(
                (1, 8, 1, rows, BLK), lambda s, table: (k, 0, table[k, 32 + 2 * s + u], 0, 0)
            )

        return [spec(u, k) for u in range(2) for k in range(2)]

    return pl.pallas_call(
        update_kernel,
        out_shape=jax.ShapeDtypeStruct((TR, TC), f32),
        grid_spec=pltpu.PrefetchScalarGridSpec(
            num_scalar_prefetch=1,
            grid=(8,),
            in_specs=[
                pl.BlockSpec((128, BLK), lambda s, table: (0, 0)),
                pl.BlockSpec((TR, 256), lambda s, table: (0, jnp.minimum(s, 3))),
                HBM,
                HBM,
                *specs(BLK),
                *specs(TOP),
                *specs(BOT),
            ],
            out_specs=pl.BlockSpec((TR, 256), lambda s, table: (0, s)),
            scratch_shapes=[
                pltpu.VMEM((TR, TR), f32),
                pltpu.VMEM((TR, TR), bf16),
                pltpu.VMEM((TR, TR), bf16),
                pltpu.VMEM((TR, 256), bf16),
                pltpu.VMEM((TR, 256), bf16),
                pltpu.SemaphoreType.DMA,
            ],
        ),
        compiler_params=pltpu.CompilerParams(vmem_limit_bytes=VMEM_LIMIT),
        name="update",
    )(
        table, diag, factors, own, came,
        *[strips.reshape(2, 8, 8, BLK, BLK)] * 4,
        *[recv.reshape(2, 8, 8, TOP, BLK)] * 4,
        *[rest.reshape(2, 8, 8, BOT, BLK)] * 4,
    )


def body(child_blocks, block_map, front_diagonal):
    diag = front_diagonal.reshape(128, BLK)
    send, rest, table = pack(block_map, child_blocks)
    recv, left, strips = exchange(send)
    rest, recv, left, strips = lax.optimization_barrier((rest, recv, left, strips))
    rest = lax.all_to_all(rest, ("row", "col"), split_axis=0, concat_axis=0, tiled=True)
    strips = strips.reshape(16, 8, BLK, BLK)
    y, factors = pivots(table, diag, recv, left, strips)
    came, recv = spread(y, send, recv)
    return update(table, diag, factors, y, came, strips, recv, rest)


def solution(mesh):
    return jax.shard_map(
        body,
        mesh=mesh,
        in_specs=(P("row", "col"), P(), P()),
        out_specs=P("row", "col"),
        check_vma=False,
    )
```

```python
import jax
import jax.numpy as jnp
from jax import lax
from jax.experimental import pallas as pl
from jax.experimental.pallas import tpu as pltpu
from jax.sharding import PartitionSpec as P

BLK = 128
PW = 512
TOP = 80
BOT = BLK - TOP
TR = 1024
TC = 2048
MESH = pl.DeviceIdType.MESH
VMEM_LIMIT = 56 * 1024 * 1024
ANY = pl.BlockSpec(memory_space=pl.ANY)
SMEM = pl.BlockSpec(memory_space=pltpu.SMEM)
VMEM = pl.BlockSpec(memory_space=pltpu.VMEM)
HBM = pl.BlockSpec(memory_space=pltpu.HBM)


def pack_kernel(map_ref, child_ref, send_ref, rest_ref, table_ref, sem, rest_sem):
    row, col = lax.axis_index("row"), lax.axis_index("col")
    child, group = row // 8, row % 8

    def start(step, carry):
        t, u = step // 8, step % 8
        q = map_ref[child, group * 8 + t] // 16
        c = map_ref[child, col * 8 + u] // 16
        block = child_ref.at[
            pl.ds(pl.multiple_of(t * BLK, BLK), BLK), pl.ds(pl.multiple_of(u * BLK, BLK), BLK)
        ]
        pltpu.make_async_copy(block, send_ref.at[q * 8 + c], sem).start()
        rest = child_ref.at[
            pl.ds(pl.multiple_of(t * BLK + TOP, 16), BOT), pl.ds(pl.multiple_of(u * BLK, BLK), BLK)
        ]
        pltpu.make_async_copy(rest, rest_ref.at[q * 16 + c], rest_sem).start()
        pltpu.make_async_copy(rest, rest_ref.at[q * 16 + 8 + c], rest_sem).start()
        return carry

    lax.fori_loop(0, 64, start, 0)

    def clear(step, carry):
        table_ref[step // 32, step % 32] = -1
        return carry

    lax.fori_loop(0, 64, clear, 0)

    def look(step, carry):
        k, s = step // 64, step % 64
        b = map_ref[k, s]

        @pl.when(b // 8 == row)
        def _():
            table_ref[k, b % 8] = s // 8

        @pl.when(b // 16 == col)
        def _():
            table_ref[k, 8 + b % 16] = s // 8

        @pl.when(b < 8)
        def _():
            table_ref[k, 24 + b] = s // 8

        return carry

    lax.fori_loop(0, 128, look, 0)
    for k in range(2):
        for j in range(16):
            here = table_ref[k, 8 + j]
            before = table_ref[k, 32 + j - 2] if j >= 2 else 0
            table_ref[k, 32 + j] = jnp.where(here >= 0, here, before)
    pltpu.make_async_copy(send_ref, send_ref, sem).wait()
    pltpu.make_async_copy(rest_ref, rest_ref, rest_sem).wait()


def pack(block_map, child):
    return pl.pallas_call(
        pack_kernel,
        out_shape=(
            jax.ShapeDtypeStruct((64, BLK, BLK), jnp.float32),
            jax.ShapeDtypeStruct((128, BOT, BLK), jnp.float32),
            jax.ShapeDtypeStruct((2, 48), jnp.int32),
        ),
        in_specs=[SMEM, VMEM],
        out_specs=(HBM, HBM, SMEM),
        scratch_shapes=[pltpu.SemaphoreType.DMA, pltpu.SemaphoreType.DMA],
        compiler_params=pltpu.CompilerParams(vmem_limit_bytes=VMEM_LIMIT),
        name="pack",
    )(block_map, child)


class Gather:
    def __init__(self, strip_ref, send_sems, recv_sems, first):
        self.strip_ref, self.send_sems, self.recv_sems, self.first = strip_ref, send_sems, recv_sems, first
        self.row, self.col = lax.axis_index("row"), lax.axis_index("col")
        x, y = self.row % 4, self.row // 4
        xl, xr, xo = (x + 3) % 4, (x + 1) % 4, (x + 2) % 4
        yl, yr, yo = (y + 3) % 4, (y + 1) % 4, (y + 2) % 4
        to = {"xr": y * 4 + xr, "xl": y * 4 + xl, "yr": yr * 4 + x, "yl": yl * 4 + x}
        lo, hi = pl.ds(0, 4), pl.ds(4, 4)
        two = [pl.ds(2 * i, 2) for i in range(4)]
        every, left, right = pl.ds(0, 4), pl.ds(0, 2), pl.ds(2, 2)
        self.steps = [
            ((y, x, lo), to["xr"], (y, xl, lo)),
            ((y, x, lo), to["xl"], (y, xr, lo)),
            ((y, x, hi), to["yr"], (yl, x, hi)),
            ((y, x, hi), to["yl"], (yr, x, hi)),
            ((y, xl, two[0]), to["xr"], (y, xo, two[0])),
            ((y, xr, two[1]), to["xl"], (y, xo, two[1])),
            ((yl, x, two[2]), to["yr"], (yo, x, two[2])),
            ((yr, x, two[3]), to["yl"], (yo, x, two[3])),
            ((y, every, lo), to["yr"], (yl, every, lo)),
            ((y, every, lo), to["yl"], (yr, every, lo)),
            ((every, x, hi), to["xr"], (every, xl, hi)),
            ((every, x, hi), to["xl"], (every, xr, hi)),
            ((yl, left, lo), to["yr"], (yo, left, lo)),
            ((yr, right, lo), to["yl"], (yo, right, lo)),
            ((left, xl, hi), to["xr"], (left, xo, hi)),
            ((right, xr, hi), to["xl"], (right, xo, hi)),
        ]

    def copy(self, step, piece, to_row):
        ref = self.strip_ref.at[piece]
        at = step - self.first
        return pltpu.make_async_remote_copy(
            ref, ref, self.send_sems.at[at], self.recv_sems.at[at],
            device_id=(to_row, self.col), device_id_type=MESH,
        )

    def go(self, *steps):
        for step in steps:
            self.copy(step, *self.steps[step][:2]).start()

    def landed(self, *steps):
        for step in steps:
            self.copy(step, self.steps[step][2], self.row).wait_recv()

    def left(self, *steps):
        for step in steps:
            self.copy(step, *self.steps[step][:2]).wait_send()

    def pass_on(self, first):
        for step in range(first, first + 4):
            self.landed(step)
            self.go(step + 4)


def exchange_kernel(
    send_ref, recv_ref, left_ref, strip_ref,
    main_s, main_r, left_s, left_r, col_s, col_r, own_sem, gat_s, gat_r,
):
    row, col = lax.axis_index("row"), lax.axis_index("col")
    me = row * 8 + col
    x, y = row % 4, row // 4
    top, bottom = pl.ds(0, TOP), pl.ds(TOP, BOT)
    own = send_ref.at[(row // 2) * 8 + col]
    own_a = pltpu.make_async_copy(own.at[top], recv_ref.at[me], own_sem.at[0])
    own_b = pltpu.make_async_copy(send_ref.at[col], strip_ref.at[y, x, col], own_sem.at[1])
    own_c = pltpu.make_async_copy(own.at[bottom], left_ref.at[me], own_sem.at[2])

    def send_strip(step, carry):
        to = (col + step) % 8
        pltpu.make_async_remote_copy(
            send_ref.at[to], strip_ref.at[y, x, col], col_s, col_r,
            device_id=(row, to), device_id_type=MESH,
        ).start()
        return carry

    def send_block(step, carry):
        to = (me + step * 45) % 128
        to_row, to_col = to // 8, to % 8
        block = send_ref.at[(to_row // 2) * 8 + to_col]
        pltpu.make_async_remote_copy(
            block.at[top], recv_ref.at[me], main_s, main_r,
            device_id=(to_row, to_col), device_id_type=MESH,
        ).start()

        @pl.when(to_col == 0)
        def _():
            pltpu.make_async_remote_copy(
                block.at[bottom], left_ref.at[me], left_s, left_r,
                device_id=(to_row, to_col), device_id_type=MESH,
            ).start()

        return carry

    own_b.start()
    lax.fori_loop(1, 8, send_strip, 0)
    own_a.start()

    @pl.when(col == 0)
    def _():
        own_c.start()

    gather = Gather(strip_ref, gat_s, gat_r, 0)
    lax.fori_loop(1, 17, send_block, 0)
    seven = strip_ref.at[y, x, pl.ds(0, 7)]
    pltpu.make_async_remote_copy(
        seven, seven, col_s, col_r, device_id=(row, col), device_id_type=MESH
    ).wait()
    own_b.wait()
    gather.go(0, 1, 2, 3)
    lax.fori_loop(17, 49, send_block, 0)
    gather.pass_on(0)
    lax.fori_loop(49, 81, send_block, 0)
    gather.landed(4, 5, 6, 7)

    @pl.when(col == 0)
    def _():
        gather.go(8, 9, 10, 11)

    lax.fori_loop(81, 105, send_block, 0)

    @pl.when(col == 0)
    def _():
        gather.pass_on(8)

    lax.fori_loop(105, 128, send_block, 0)
    gather.left(*range(8))

    def blocks(ref, count, send_sem, recv_sem):
        part = ref.at[pl.ds(0, count)]
        return pltpu.make_async_remote_copy(
            part, part, send_sem, recv_sem, device_id=(row, col), device_id_type=MESH
        )

    @pl.when(col == 0)
    def _():
        gather.landed(12, 13, 14, 15)
        gather.left(*range(8, 16))
        own_c.wait()
        blocks(left_ref, 15, left_s, left_r).wait_send()
        blocks(left_ref, 127, left_s, left_r).wait_recv()

    @pl.when(col > 0)
    def _():
        blocks(left_ref, 16, left_s, left_r).wait_send()

    own_a.wait()
    blocks(recv_ref, 127, main_s, main_r).wait()


def exchange(send):
    dma = pltpu.SemaphoreType.DMA
    return pl.pallas_call(
        exchange_kernel,
        out_shape=(
            jax.ShapeDtypeStruct((128, TOP, BLK), jnp.float32),
            jax.ShapeDtypeStruct((128, BOT, BLK), jnp.float32),
            jax.ShapeDtypeStruct((4, 4, 8, BLK, BLK), jnp.float32),
        ),
        in_specs=[HBM],
        out_specs=(HBM, HBM, HBM),
        scratch_shapes=[dma, dma, dma, dma, dma, dma, dma((3,)), dma((16,)), dma((16,))],
        compiler_params=pltpu.CompilerParams(has_side_effects=True, vmem_limit_bytes=VMEM_LIMIT),
        name="exchange",
    )(send)


def split(value):
    high = value.astype(jnp.bfloat16)
    return high, (value - high.astype(jnp.float32)).astype(jnp.bfloat16)


def dot1(a, b):
    return jnp.dot(a, b, preferred_element_type=jnp.float32)


def dot3(a, b):
    return dot1(a[0], b[0]) + (dot1(a[0], b[1]) + dot1(a[1], b[0]))


def identity(n):
    return lax.broadcasted_iota(jnp.int32, (n, n), 0) == lax.broadcasted_iota(jnp.int32, (n, n), 1)


def inverse_into(matrix_ref, scaled_ref, x_ref, out_ref):
    eye = identity(PW)
    matrix = matrix_ref[...]
    diagonal = jnp.where(eye, matrix, 0.0)
    by_col = lax.rsqrt(jnp.sum(diagonal, axis=0, keepdims=True))
    by_row = lax.rsqrt(jnp.sum(diagonal, axis=1, keepdims=True))
    scaled = matrix * by_row * by_col
    scaled_ref[...] = scaled
    bound = jnp.max(jnp.sum(jnp.abs(scaled), axis=0, keepdims=True))
    alpha = jnp.minimum(1.0, 1.9 / bound)

    def begin():
        x_ref[...] = jnp.where(eye, 2.0 * alpha, 0.0) - alpha * alpha * scaled_ref[...]

    def run(most, settled, first, second):
        def step(carry):
            count, _ = carry
            value = x_ref[...]
            residual = jnp.where(eye, 1.0, 0.0) - first(scaled_ref[...], value)
            x_ref[...] += second(value, residual)
            return count + 1, jnp.sum(residual * residual)

        return lax.while_loop(
            lambda carry: (carry[0] < most) & (carry[1] > settled), step, (jnp.int32(0), jnp.float32(1e9))
        )[1]

    def once(a, b):
        return dot1(a.astype(jnp.bfloat16), b.astype(jnp.bfloat16))

    def thrice(a, b):
        return dot3(split(a), split(b))

    begin()
    run(10, 1.0, once, once)
    left = run(5, 1e-6, thrice, once)

    @pl.when(jnp.logical_not(left <= 1e-6))
    def _():
        begin()
        run(48, 1e-6, thrice, thrice)

    residual = jnp.where(eye, 1.0, 0.0) - jnp.dot(
        scaled_ref[...], x_ref[...], precision=lax.Precision.HIGHEST, preferred_element_type=jnp.float32
    )
    value = x_ref[...]
    value = value + thrice(value, residual)
    out_ref[...] = value * by_row * by_col


def pivot_kernel(
    table_ref, diag_ref, recv_ref, left_ref, strip_ref, y_ref, f_ref,
    strips, blocks, piv, tile, inv0, inv1, l10, scaled, newton, schur, sems,
):
    row, col = lax.axis_index("row"), lax.axis_index("col")

    @pl.when(col == 0)
    def _():
        load_a = pltpu.make_async_copy(strip_ref, strips, sems.at[0])
        load_b = pltpu.make_async_copy(recv_ref, blocks.at[:, pl.ds(0, TOP)], sems.at[1])
        load_c = pltpu.make_async_copy(left_ref, blocks.at[:, pl.ds(TOP, BOT)], sems.at[2])
        load_a.start()
        load_b.start()
        load_c.start()
        load_a.wait()

        def pivot_block(step, carry):
            a, b = step // 8, step % 8
            total = jnp.where(identity(BLK) & (a == b), diag_ref[pl.ds(a, 1), :], 0.0)
            for k in range(2):
                ga, gb = table_ref[k, 24 + a], table_ref[k, 24 + b]
                value = strips[k * 8 + jnp.maximum(ga, 0), jnp.maximum(gb, 0)]
                total = total + jnp.where((ga >= 0) & (gb >= 0), value, 0.0)
            piv[pl.ds(pl.multiple_of(a * BLK, BLK), BLK), pl.ds(pl.multiple_of(b * BLK, BLK), BLK)] = total
            return carry

        lax.fori_loop(0, 64, pivot_block, 0)
        schur[...] = piv[:PW, :PW]
        inverse_into(schur, scaled, newton, inv0)
        l10[...] = dot3(split(piv[PW:, :PW]), split(inv0[...]))
        schur[...] = piv[PW:, PW:] - dot3(split(l10[...]), split(piv[:PW, PW:]))

        load_b.wait()
        load_c.wait()

        @pl.when(row == 0)
        def _():
            f_ref[:PW, :] = piv[:PW, :]
            f_ref[PW:, :PW] = l10[...]
            f_ref[PW:, PW:] = schur[...]
            y_ref[...] = jnp.zeros((TR, TR), jnp.float32)
            y_ref[PW:, :PW] = l10[...]

        @pl.when(row > 0)
        def _():
            inverse_into(schur, scaled, newton, inv1)

            def tile_block(step, carry):
                a, b = step // 8, step % 8
                total = jnp.zeros((BLK, BLK), jnp.float32)
                for k in range(2):
                    ga, hb = table_ref[k, a], table_ref[k, 24 + b]
                    value = blocks[k * 64 + jnp.maximum(ga, 0) * 8 + jnp.maximum(hb, 0)]
                    total = total + jnp.where((ga >= 0) & (hb >= 0), value, 0.0)
                tile[pl.ds(pl.multiple_of(a * BLK, BLK), BLK), pl.ds(pl.multiple_of(b * BLK, BLK), BLK)] = total
                return carry

            lax.fori_loop(0, 64, tile_block, 0)
            for part in range(2):
                rows = pl.ds(part * PW, PW)
                factor0 = dot3(split(tile[rows, :PW]), split(inv0[...]))
                f_ref[rows, :PW] = factor0
                rest = tile[rows, PW:] - dot3(split(factor0), split(piv[:PW, PW:]))
                factor1 = dot3(split(rest), split(inv1[...]))
                f_ref[rows, PW:] = factor1
                y_ref[rows, PW:] = factor1
                y_ref[rows, :PW] = f_ref[rows, :PW] - dot3(split(factor1), split(l10[...]))


def pivots(table, diag, recv, left, strips):
    f32 = jnp.float32
    half = pltpu.VMEM((PW, PW), f32)
    return pl.pallas_call(
        pivot_kernel,
        out_shape=(jax.ShapeDtypeStruct((TR, TR), f32), jax.ShapeDtypeStruct((TR, TR), f32)),
        in_specs=[SMEM, VMEM, HBM, HBM, HBM],
        out_specs=(VMEM, VMEM),
        scratch_shapes=[
            pltpu.VMEM((16, 8, BLK, BLK), f32),
            pltpu.VMEM((128, BLK, BLK), f32),
            pltpu.VMEM((TR, TR), f32),
            pltpu.VMEM((TR, TR), f32),
            half, half, half, half, half, half,
            pltpu.SemaphoreType.DMA((3,)),
        ],
        compiler_params=pltpu.CompilerParams(vmem_limit_bytes=VMEM_LIMIT),
        name="pivots",
    )(table, diag, recv, left, strips)


CHUNKS = 16
WINDOW = 4
PASS = 10


def spread_kernel(
    y_ref, _, out_ref, strip_ref, ring_s, ring_r, core_s, core_r, gat_s, gat_r
):
    row, col = lax.axis_index("row"), lax.axis_index("col")
    z, core = col // 2, col % 2
    size = TR // CHUNKS

    def ring(source, t):
        step = 1 if t % 2 == 0 else 3
        rows = pl.ds(t * size, size)
        return pltpu.make_async_remote_copy(
            source.at[rows], out_ref.at[rows], ring_s.at[t], ring_r.at[t],
            device_id=(row, ((z + step) % 4) * 2), device_id_type=MESH,
        )

    def across(source, t):
        rows = pl.ds(t * size, size)
        return pltpu.make_async_remote_copy(
            source.at[rows], out_ref.at[rows], core_s.at[t], core_r.at[t],
            device_id=(row, z * 2 + 1), device_id_type=MESH,
        )

    gather = Gather(strip_ref, gat_s, gat_r, 8)

    @pl.when(col != 0)
    def _():
        gather.go(8, 9, 10, 11)

    @pl.when(col == 0)
    def _():
        for t in range(CHUNKS):
            if t >= WINDOW:
                ring(y_ref, t - WINDOW).wait_send()
            ring(y_ref, t).start()
            across(y_ref, t).start()
        for t in range(CHUNKS):
            if t >= CHUNKS - WINDOW:
                ring(y_ref, t).wait_send()
            across(y_ref, t).wait_send()

    def relay(place):
        def goes(t):
            return place != (3 if t % 2 == 0 else 1)

        order = sorted(range(CHUNKS), key=lambda t: (not goes(t), t))
        for n, t in enumerate(order):
            ring(out_ref, t).wait_recv()
            if goes(t):
                ring(out_ref, t).start()
            across(out_ref, t).start()
            if n == PASS:
                gather.pass_on(8)
        for t in range(CHUNKS):
            if goes(t):
                ring(out_ref, t).wait_send()
            across(out_ref, t).wait_send()

    for place in range(1, 4):

        @pl.when((core == 0) & (z == place))
        def _(place=place):
            relay(place)

    @pl.when(core == 1)
    def _():
        gather.pass_on(8)
        for t in range(CHUNKS):
            across(out_ref, t).wait_recv()

    @pl.when(col != 0)
    def _():
        gather.landed(12, 13, 14, 15)
        gather.left(*range(8, 16))


def spread(y, strips):
    dma = pltpu.SemaphoreType.DMA
    return pl.pallas_call(
        spread_kernel,
        out_shape=(
            jax.ShapeDtypeStruct((TR, TR), jnp.float32),
            jax.ShapeDtypeStruct((4, 4, 8, BLK, BLK), jnp.float32),
        ),
        in_specs=[HBM, HBM],
        out_specs=(HBM, HBM),
        input_output_aliases={1: 1},
        scratch_shapes=[
            dma((CHUNKS,)), dma((CHUNKS,)), dma((CHUNKS,)), dma((CHUNKS,)), dma((8,)), dma((8,)),
        ],
        compiler_params=pltpu.CompilerParams(has_side_effects=True, vmem_limit_bytes=VMEM_LIMIT),
        name="spread",
    )(y, strips)


def update_kernel(table_ref, diag_ref, f_ref, own_ref, came_ref, *refs):
    strips, tops, bottoms = refs[0:4], refs[4:8], refs[8:12]
    out_ref, y, yc, uc, sem = refs[12:]
    row, col = lax.axis_index("row"), lax.axis_index("col")
    step = pl.program_id(0)

    @pl.when(step == 0)
    def _():
        @pl.when(col == 0)
        def _():
            copy = pltpu.make_async_copy(own_ref, y, sem)
            copy.start()
            copy.wait()

        @pl.when(col != 0)
        def _():
            copy = pltpu.make_async_copy(came_ref, y, sem)
            copy.start()
            copy.wait()

        yc[:, :TR], yc[:, 2 * TR :] = split(y[...])
        yc[:, TR : 2 * TR] = yc[:, :TR]

    factors = (col == 0) & (step < 4)

    @pl.when(factors)
    def _():
        out_ref[...] = f_ref[...]

    @pl.when(jnp.logical_not(factors))
    def _():
        for u in range(2):
            j = step * 2 + u

            def strip_block(i):
                on = identity(BLK) & (col * 16 + j == i)
                total = jnp.where(on, diag_ref[pl.ds(i, 1), :], 0.0)
                for k in range(2):
                    g, h = table_ref[k, 24 + i], table_ref[k, 8 + j]
                    value = strips[2 * u + k][0, jnp.maximum(g, 0), 0]
                    total = total + jnp.where((g >= 0) & (h >= 0), value, 0.0)
                high, low = split(total)
                for part, value in enumerate((high, low, high)):
                    uc[pl.ds(part * TR + i * BLK, BLK), pl.ds(u * BLK, BLK)] = value

            for i in range(8):
                strip_block(i)

        out_ref[...] = dot1(yc[...], uc[...])
        for u in range(2):
            j = step * 2 + u

            def front_block(i):
                for refs, first, count in ((tops, 0, TOP), (bottoms, TOP, BOT)):
                    there = lax.broadcasted_iota(jnp.int32, (count, BLK), 0) + first
                    on = (there == lax.broadcasted_iota(jnp.int32, (count, BLK), 1)) & (
                        col * 16 + j == row * 8 + i
                    )
                    total = jnp.where(on, diag_ref[pl.ds(row * 8 + i, 1), :], 0.0)
                    for k in range(2):
                        g, h = table_ref[k, i], table_ref[k, 8 + j]
                        value = refs[2 * u + k][0, jnp.maximum(g, 0), 0]
                        total = total + jnp.where((g >= 0) & (h >= 0), value, 0.0)
                    at = pl.ds(i * BLK + first, count), pl.ds(u * BLK, BLK)
                    out_ref[at] = total - out_ref[at]

            for i in range(8):
                front_block(i)


def update(table, diag, factors, own, came, strips, recv, rest):
    f32, bf16 = jnp.float32, jnp.bfloat16

    def specs(rows):
        def spec(u, k):
            return pl.BlockSpec(
                (1, 8, 1, rows, BLK), lambda s, table: (k, 0, table[k, 32 + 2 * s + u], 0, 0)
            )

        return [spec(u, k) for u in range(2) for k in range(2)]

    return pl.pallas_call(
        update_kernel,
        out_shape=jax.ShapeDtypeStruct((TR, TC), f32),
        grid_spec=pltpu.PrefetchScalarGridSpec(
            num_scalar_prefetch=1,
            grid=(8,),
            in_specs=[
                pl.BlockSpec((128, BLK), lambda s, table: (0, 0)),
                pl.BlockSpec((TR, 256), lambda s, table: (0, jnp.minimum(s, 3))),
                HBM,
                HBM,
                *specs(BLK),
                *specs(TOP),
                *specs(BOT),
            ],
            out_specs=pl.BlockSpec((TR, 256), lambda s, table: (0, s)),
            scratch_shapes=[
                pltpu.VMEM((TR, TR), f32),
                pltpu.VMEM((TR, 3 * TR), bf16),
                pltpu.VMEM((3 * TR, 256), bf16),
                pltpu.SemaphoreType.DMA,
            ],
        ),
        compiler_params=pltpu.CompilerParams(vmem_limit_bytes=VMEM_LIMIT),
        name="update",
    )(
        table, diag, factors, own, came,
        *[strips.reshape(2, 8, 8, BLK, BLK)] * 4,
        *[recv.reshape(2, 8, 8, TOP, BLK)] * 4,
        *[rest.reshape(2, 8, 8, BOT, BLK)] * 4,
    )


def body(child_blocks, block_map, front_diagonal):
    diag = front_diagonal.reshape(128, BLK)
    send, rest, table = pack(block_map, child_blocks)
    recv, left, strips = exchange(send)
    rest, recv, left, strips = lax.optimization_barrier((rest, recv, left, strips))
    rest = lax.all_to_all(rest, ("row", "col"), split_axis=0, concat_axis=0, tiled=True)
    y, factors = pivots(table, diag, recv, left, strips.reshape(16, 8, BLK, BLK))
    came, strips = spread(y, strips)
    return update(table, diag, factors, y, came, strips, recv, rest)


def solution(mesh):
    return jax.shard_map(
        body,
        mesh=mesh,
        in_specs=(P("row", "col"), P(), P()),
        out_specs=P("row", "col"),
        check_vma=False,
    )
```

```python
import jax
import jax.numpy as jnp
from jax import lax
from jax.experimental import pallas as pl
from jax.experimental.pallas import tpu as pltpu
from jax.sharding import PartitionSpec as P

BLK = 128
PW = 512
TOP = 64
BOT = BLK - TOP
TR = 1024
TC = 2048
MESH = pl.DeviceIdType.MESH
VMEM_LIMIT = 56 * 1024 * 1024
ANY = pl.BlockSpec(memory_space=pl.ANY)
SMEM = pl.BlockSpec(memory_space=pltpu.SMEM)
VMEM = pl.BlockSpec(memory_space=pltpu.VMEM)
HBM = pl.BlockSpec(memory_space=pltpu.HBM)


def pack_kernel(map_ref, child_ref, send_ref, rest_ref, table_ref, sem, rest_sem):
    row, col = lax.axis_index("row"), lax.axis_index("col")
    child, group = row // 8, row % 8

    def start(step, carry):
        t, u = step // 8, step % 8
        q = map_ref[child, group * 8 + t] // 16
        c = map_ref[child, col * 8 + u] // 16
        block = child_ref.at[
            pl.ds(pl.multiple_of(t * BLK, BLK), BLK), pl.ds(pl.multiple_of(u * BLK, BLK), BLK)
        ]
        pltpu.make_async_copy(block, send_ref.at[q * 8 + c], sem).start()
        rest = child_ref.at[
            pl.ds(pl.multiple_of(t * BLK + TOP, 16), BOT), pl.ds(pl.multiple_of(u * BLK, BLK), BLK)
        ]
        pltpu.make_async_copy(rest, rest_ref.at[q * 16 + c], rest_sem).start()
        pltpu.make_async_copy(rest, rest_ref.at[q * 16 + 8 + c], rest_sem).start()
        return carry

    lax.fori_loop(0, 64, start, 0)

    def clear(step, carry):
        table_ref[step // 32, step % 32] = -1
        return carry

    lax.fori_loop(0, 64, clear, 0)

    def look(step, carry):
        k, s = step // 64, step % 64
        b = map_ref[k, s]

        @pl.when(b // 8 == row)
        def _():
            table_ref[k, b % 8] = s // 8

        @pl.when(b // 16 == col)
        def _():
            table_ref[k, 8 + b % 16] = s // 8

        @pl.when(b < 8)
        def _():
            table_ref[k, 24 + b] = s // 8

        return carry

    lax.fori_loop(0, 128, look, 0)
    for k in range(2):
        for j in range(16):
            here = table_ref[k, 8 + j]
            before = table_ref[k, 32 + j - 2] if j >= 2 else 0
            table_ref[k, 32 + j] = jnp.where(here >= 0, here, before)
    pltpu.make_async_copy(send_ref, send_ref, sem).wait()
    pltpu.make_async_copy(rest_ref, rest_ref, rest_sem).wait()


def pack(block_map, child):
    return pl.pallas_call(
        pack_kernel,
        out_shape=(
            jax.ShapeDtypeStruct((64, BLK, BLK), jnp.float32),
            jax.ShapeDtypeStruct((128, BOT, BLK), jnp.float32),
            jax.ShapeDtypeStruct((2, 48), jnp.int32),
        ),
        in_specs=[SMEM, VMEM],
        out_specs=(HBM, HBM, SMEM),
        scratch_shapes=[pltpu.SemaphoreType.DMA, pltpu.SemaphoreType.DMA],
        compiler_params=pltpu.CompilerParams(vmem_limit_bytes=VMEM_LIMIT),
        name="pack",
    )(block_map, child)


class Gather:
    def __init__(self, strip_ref, send_sems, recv_sems, first):
        self.strip_ref, self.send_sems, self.recv_sems, self.first = strip_ref, send_sems, recv_sems, first
        self.row, self.col = lax.axis_index("row"), lax.axis_index("col")
        x, y = self.row % 4, self.row // 4
        xl, xr, xo = (x + 3) % 4, (x + 1) % 4, (x + 2) % 4
        yl, yr, yo = (y + 3) % 4, (y + 1) % 4, (y + 2) % 4
        to = {"xr": y * 4 + xr, "xl": y * 4 + xl, "yr": yr * 4 + x, "yl": yl * 4 + x}
        lo, hi = pl.ds(0, 4), pl.ds(4, 4)
        two = [pl.ds(2 * i, 2) for i in range(4)]
        every, left, right = pl.ds(0, 4), pl.ds(0, 2), pl.ds(2, 2)
        self.steps = [
            ((y, x, lo), to["xr"], (y, xl, lo)),
            ((y, x, lo), to["xl"], (y, xr, lo)),
            ((y, x, hi), to["yr"], (yl, x, hi)),
            ((y, x, hi), to["yl"], (yr, x, hi)),
            ((y, xl, two[0]), to["xr"], (y, xo, two[0])),
            ((y, xr, two[1]), to["xl"], (y, xo, two[1])),
            ((yl, x, two[2]), to["yr"], (yo, x, two[2])),
            ((yr, x, two[3]), to["yl"], (yo, x, two[3])),
            ((y, every, lo), to["yr"], (yl, every, lo)),
            ((y, every, lo), to["yl"], (yr, every, lo)),
            ((every, x, hi), to["xr"], (every, xl, hi)),
            ((every, x, hi), to["xl"], (every, xr, hi)),
            ((yl, left, lo), to["yr"], (yo, left, lo)),
            ((yr, right, lo), to["yl"], (yo, right, lo)),
            ((left, xl, hi), to["xr"], (left, xo, hi)),
            ((right, xr, hi), to["xl"], (right, xo, hi)),
        ]

    def copy(self, step, piece, to_row):
        ref = self.strip_ref.at[piece]
        at = step - self.first
        return pltpu.make_async_remote_copy(
            ref, ref, self.send_sems.at[at], self.recv_sems.at[at],
            device_id=(to_row, self.col), device_id_type=MESH,
        )

    def go(self, *steps):
        for step in steps:
            self.copy(step, *self.steps[step][:2]).start()

    def landed(self, *steps):
        for step in steps:
            self.copy(step, self.steps[step][2], self.row).wait_recv()

    def left(self, *steps):
        for step in steps:
            self.copy(step, *self.steps[step][:2]).wait_send()

    def pass_on(self, first):
        for step in range(first, first + 4):
            self.landed(step)
            self.go(step + 4)


def exchange_kernel(
    send_ref, recv_ref, left_ref, strip_ref,
    main_s, main_r, left_s, left_r, col_s, col_r, own_sem, gat_s, gat_r,
):
    row, col = lax.axis_index("row"), lax.axis_index("col")
    me = row * 8 + col
    x, y = row % 4, row // 4
    top, bottom = pl.ds(0, TOP), pl.ds(TOP, BOT)
    own = send_ref.at[(row // 2) * 8 + col]
    own_a = pltpu.make_async_copy(own.at[top], recv_ref.at[me], own_sem.at[0])
    own_b = pltpu.make_async_copy(send_ref.at[col], strip_ref.at[y, x, col], own_sem.at[1])
    own_c = pltpu.make_async_copy(own.at[bottom], left_ref.at[me], own_sem.at[2])

    def send_strip(step, carry):
        to = (col + step) % 8
        pltpu.make_async_remote_copy(
            send_ref.at[to], strip_ref.at[y, x, col], col_s, col_r,
            device_id=(row, to), device_id_type=MESH,
        ).start()
        return carry

    def send_block(step, carry):
        way = (step * 37) % 128
        to_row = ((y + way // 4) % 4) * 4 + (x + way) % 4
        to_col = ((col // 2 + way // 16) % 4) * 2 + (col + way // 64) % 2
        block = send_ref.at[(to_row // 2) * 8 + to_col]
        pltpu.make_async_remote_copy(
            block.at[top], recv_ref.at[me], main_s, main_r,
            device_id=(to_row, to_col), device_id_type=MESH,
        ).start()

        @pl.when(to_col == 0)
        def _():
            pltpu.make_async_remote_copy(
                block.at[bottom], left_ref.at[me], left_s, left_r,
                device_id=(to_row, to_col), device_id_type=MESH,
            ).start()

        return carry

    own_b.start()
    lax.fori_loop(1, 8, send_strip, 0)
    own_a.start()

    @pl.when(col == 0)
    def _():
        own_c.start()

    gather = Gather(strip_ref, gat_s, gat_r, 0)
    lax.fori_loop(1, 17, send_block, 0)
    seven = strip_ref.at[y, x, pl.ds(0, 7)]
    pltpu.make_async_remote_copy(
        seven, seven, col_s, col_r, device_id=(row, col), device_id_type=MESH
    ).wait()
    own_b.wait()
    gather.go(0, 1, 2, 3)
    lax.fori_loop(17, 49, send_block, 0)
    gather.pass_on(0)
    lax.fori_loop(49, 81, send_block, 0)
    gather.landed(4, 5, 6, 7)

    @pl.when(col == 0)
    def _():
        gather.go(8, 9, 10, 11)

    lax.fori_loop(81, 105, send_block, 0)

    @pl.when(col == 0)
    def _():
        gather.pass_on(8)

    lax.fori_loop(105, 128, send_block, 0)
    gather.left(*range(8))

    def blocks(ref, count, send_sem, recv_sem):
        part = ref.at[pl.ds(0, count)]
        return pltpu.make_async_remote_copy(
            part, part, send_sem, recv_sem, device_id=(row, col), device_id_type=MESH
        )

    @pl.when(col == 0)
    def _():
        gather.landed(12, 13, 14, 15)
        gather.left(*range(8, 16))
        own_c.wait()
        blocks(left_ref, 15, left_s, left_r).wait_send()
        blocks(left_ref, 127, left_s, left_r).wait_recv()

    @pl.when(col > 0)
    def _():
        blocks(left_ref, 16, left_s, left_r).wait_send()

    own_a.wait()
    blocks(recv_ref, 127, main_s, main_r).wait()


def exchange(send):
    dma = pltpu.SemaphoreType.DMA
    return pl.pallas_call(
        exchange_kernel,
        out_shape=(
            jax.ShapeDtypeStruct((128, TOP, BLK), jnp.float32),
            jax.ShapeDtypeStruct((128, BOT, BLK), jnp.float32),
            jax.ShapeDtypeStruct((4, 4, 8, BLK, BLK), jnp.float32),
        ),
        in_specs=[HBM],
        out_specs=(HBM, HBM, HBM),
        scratch_shapes=[dma, dma, dma, dma, dma, dma, dma((3,)), dma((16,)), dma((16,))],
        compiler_params=pltpu.CompilerParams(has_side_effects=True, vmem_limit_bytes=VMEM_LIMIT),
        name="exchange",
    )(send)


def split(value):
    high = value.astype(jnp.bfloat16)
    return high, (value - high.astype(jnp.float32)).astype(jnp.bfloat16)


def dot1(a, b):
    return jnp.dot(a, b, preferred_element_type=jnp.float32)


def dot3(a, b):
    return dot1(a[0], b[0]) + (dot1(a[0], b[1]) + dot1(a[1], b[0]))


def identity(n):
    return lax.broadcasted_iota(jnp.int32, (n, n), 0) == lax.broadcasted_iota(jnp.int32, (n, n), 1)


def inverse_into(matrix_ref, scaled_ref, x_ref, out_ref):
    eye = identity(PW)
    matrix = matrix_ref[...]
    diagonal = jnp.where(eye, matrix, 0.0)
    by_col = lax.rsqrt(jnp.sum(diagonal, axis=0, keepdims=True))
    by_row = lax.rsqrt(jnp.sum(diagonal, axis=1, keepdims=True))
    scaled = matrix * by_row * by_col
    scaled_ref[...] = scaled
    bound = jnp.max(jnp.sum(jnp.abs(scaled), axis=0, keepdims=True))
    alpha = jnp.minimum(1.0, 1.9 / bound)

    def begin():
        x_ref[...] = jnp.where(eye, 2.0 * alpha, 0.0) - alpha * alpha * scaled_ref[...]

    def run(most, settled, first, second):
        def step(carry):
            count, _ = carry
            value = x_ref[...]
            residual = jnp.where(eye, 1.0, 0.0) - first(scaled_ref[...], value)
            x_ref[...] += second(value, residual)
            return count + 1, jnp.sum(residual * residual)

        return lax.while_loop(
            lambda carry: (carry[0] < most) & (carry[1] > settled), step, (jnp.int32(0), jnp.float32(1e9))
        )[1]

    def once(a, b):
        return dot1(a.astype(jnp.bfloat16), b.astype(jnp.bfloat16))

    def thrice(a, b):
        return dot3(split(a), split(b))

    begin()
    run(10, 1.0, once, once)
    left = run(5, 1e-6, thrice, once)

    @pl.when(jnp.logical_not(left <= 1e-6))
    def _():
        begin()
        run(48, 1e-6, thrice, thrice)

    residual = jnp.where(eye, 1.0, 0.0) - jnp.dot(
        scaled_ref[...], x_ref[...], precision=lax.Precision.HIGHEST, preferred_element_type=jnp.float32
    )
    value = x_ref[...]
    value = value + thrice(value, residual)
    out_ref[...] = value * by_row * by_col


def pivot_kernel(
    table_ref, diag_ref, recv_ref, left_ref, strip_ref, y_ref, f_ref,
    strips, blocks, piv, tile, inv0, inv1, l10, scaled, newton, schur, sems,
):
    row, col = lax.axis_index("row"), lax.axis_index("col")

    @pl.when(col == 0)
    def _():
        load_a = pltpu.make_async_copy(strip_ref, strips, sems.at[0])
        load_b = pltpu.make_async_copy(recv_ref, blocks.at[:, pl.ds(0, TOP)], sems.at[1])
        load_c = pltpu.make_async_copy(left_ref, blocks.at[:, pl.ds(TOP, BOT)], sems.at[2])
        load_a.start()
        load_b.start()
        load_c.start()
        load_a.wait()

        def pivot_block(step, carry):
            a, b = step // 8, step % 8
            total = jnp.where(identity(BLK) & (a == b), diag_ref[pl.ds(a, 1), :], 0.0)
            for k in range(2):
                ga, gb = table_ref[k, 24 + a], table_ref[k, 24 + b]
                value = strips[k * 8 + jnp.maximum(ga, 0), jnp.maximum(gb, 0)]
                total = total + jnp.where((ga >= 0) & (gb >= 0), value, 0.0)
            piv[pl.ds(pl.multiple_of(a * BLK, BLK), BLK), pl.ds(pl.multiple_of(b * BLK, BLK), BLK)] = total
            return carry

        lax.fori_loop(0, 64, pivot_block, 0)
        schur[...] = piv[:PW, :PW]
        inverse_into(schur, scaled, newton, inv0)
        l10[...] = dot3(split(piv[PW:, :PW]), split(inv0[...]))
        schur[...] = piv[PW:, PW:] - dot3(split(l10[...]), split(piv[:PW, PW:]))

        load_b.wait()
        load_c.wait()

        @pl.when(row == 0)
        def _():
            f_ref[:PW, :] = piv[:PW, :]
            f_ref[PW:, :PW] = l10[...]
            f_ref[PW:, PW:] = schur[...]
            y_ref[...] = jnp.zeros((TR, TR), jnp.float32)
            y_ref[PW:, :PW] = l10[...]

        @pl.when(row > 0)
        def _():
            inverse_into(schur, scaled, newton, inv1)

            def tile_block(step, carry):
                a, b = step // 8, step % 8
                total = jnp.zeros((BLK, BLK), jnp.float32)
                for k in range(2):
                    ga, hb = table_ref[k, a], table_ref[k, 24 + b]
                    value = blocks[k * 64 + jnp.maximum(ga, 0) * 8 + jnp.maximum(hb, 0)]
                    total = total + jnp.where((ga >= 0) & (hb >= 0), value, 0.0)
                tile[pl.ds(pl.multiple_of(a * BLK, BLK), BLK), pl.ds(pl.multiple_of(b * BLK, BLK), BLK)] = total
                return carry

            lax.fori_loop(0, 64, tile_block, 0)
            for part in range(2):
                rows = pl.ds(part * PW, PW)
                factor0 = dot3(split(tile[rows, :PW]), split(inv0[...]))
                f_ref[rows, :PW] = factor0
                rest = tile[rows, PW:] - dot3(split(factor0), split(piv[:PW, PW:]))
                factor1 = dot3(split(rest), split(inv1[...]))
                f_ref[rows, PW:] = factor1
                y_ref[rows, PW:] = factor1
                y_ref[rows, :PW] = f_ref[rows, :PW] - dot3(split(factor1), split(l10[...]))


def pivots(table, diag, recv, left, strips):
    f32 = jnp.float32
    half = pltpu.VMEM((PW, PW), f32)
    return pl.pallas_call(
        pivot_kernel,
        out_shape=(jax.ShapeDtypeStruct((TR, TR), f32), jax.ShapeDtypeStruct((TR, TR), f32)),
        in_specs=[SMEM, VMEM, HBM, HBM, HBM],
        out_specs=(VMEM, VMEM),
        scratch_shapes=[
            pltpu.VMEM((16, 8, BLK, BLK), f32),
            pltpu.VMEM((128, BLK, BLK), f32),
            pltpu.VMEM((TR, TR), f32),
            pltpu.VMEM((TR, TR), f32),
            half, half, half, half, half, half,
            pltpu.SemaphoreType.DMA((3,)),
        ],
        compiler_params=pltpu.CompilerParams(vmem_limit_bytes=VMEM_LIMIT),
        name="pivots",
    )(table, diag, recv, left, strips)


CHUNKS = 16
WINDOW = 4
PASS = 10


def spread_kernel(
    y_ref, _, out_ref, strip_ref, ring_s, ring_r, core_s, core_r, gat_s, gat_r
):
    row, col = lax.axis_index("row"), lax.axis_index("col")
    z, core = col // 2, col % 2
    size = TR // CHUNKS

    def ring(source, t):
        step = 1 if t % 2 == 0 else 3
        rows = pl.ds(t * size, size)
        return pltpu.make_async_remote_copy(
            source.at[rows], out_ref.at[rows], ring_s.at[t], ring_r.at[t],
            device_id=(row, ((z + step) % 4) * 2), device_id_type=MESH,
        )

    def across(source, t):
        rows = pl.ds(t * size, size)
        return pltpu.make_async_remote_copy(
            source.at[rows], out_ref.at[rows], core_s.at[t], core_r.at[t],
            device_id=(row, z * 2 + 1), device_id_type=MESH,
        )

    gather = Gather(strip_ref, gat_s, gat_r, 8)

    @pl.when(col != 0)
    def _():
        gather.go(8, 9, 10, 11)

    @pl.when(col == 0)
    def _():
        for t in range(CHUNKS):
            if t >= WINDOW:
                ring(y_ref, t - WINDOW).wait_send()
            ring(y_ref, t).start()
            across(y_ref, t).start()
        for t in range(CHUNKS):
            if t >= CHUNKS - WINDOW:
                ring(y_ref, t).wait_send()
            across(y_ref, t).wait_send()

    def relay(place):
        def goes(t):
            return place != (3 if t % 2 == 0 else 1)

        order = sorted(range(CHUNKS), key=lambda t: (not goes(t), t))
        for n, t in enumerate(order):
            ring(out_ref, t).wait_recv()
            if goes(t):
                ring(out_ref, t).start()
            across(out_ref, t).start()
            if n == PASS:
                gather.pass_on(8)
        for t in range(CHUNKS):
            if goes(t):
                ring(out_ref, t).wait_send()
            across(out_ref, t).wait_send()

    for place in range(1, 4):

        @pl.when((core == 0) & (z == place))
        def _(place=place):
            relay(place)

    @pl.when(core == 1)
    def _():
        gather.pass_on(8)
        for t in range(CHUNKS):
            across(out_ref, t).wait_recv()

    @pl.when(col != 0)
    def _():
        gather.landed(12, 13, 14, 15)
        gather.left(*range(8, 16))


def spread(y, strips):
    dma = pltpu.SemaphoreType.DMA
    return pl.pallas_call(
        spread_kernel,
        out_shape=(
            jax.ShapeDtypeStruct((TR, TR), jnp.float32),
            jax.ShapeDtypeStruct((4, 4, 8, BLK, BLK), jnp.float32),
        ),
        in_specs=[HBM, HBM],
        out_specs=(HBM, HBM),
        input_output_aliases={1: 1},
        scratch_shapes=[
            dma((CHUNKS,)), dma((CHUNKS,)), dma((CHUNKS,)), dma((CHUNKS,)), dma((8,)), dma((8,)),
        ],
        compiler_params=pltpu.CompilerParams(has_side_effects=True, vmem_limit_bytes=VMEM_LIMIT),
        name="spread",
    )(y, strips)


def update_kernel(table_ref, diag_ref, f_ref, own_ref, came_ref, *refs):
    strips, tops, bottoms = refs[0:4], refs[4:8], refs[8:12]
    out_ref, y, yc, uc, sem = refs[12:]
    row, col = lax.axis_index("row"), lax.axis_index("col")
    step = pl.program_id(0)

    @pl.when(step == 0)
    def _():
        @pl.when(col == 0)
        def _():
            copy = pltpu.make_async_copy(own_ref, y, sem)
            copy.start()
            copy.wait()

        @pl.when(col != 0)
        def _():
            copy = pltpu.make_async_copy(came_ref, y, sem)
            copy.start()
            copy.wait()

        yc[:, :TR], yc[:, 2 * TR :] = split(y[...])
        yc[:, TR : 2 * TR] = yc[:, :TR]

    factors = (col == 0) & (step < 4)

    @pl.when(factors)
    def _():
        out_ref[...] = f_ref[...]

    @pl.when(jnp.logical_not(factors))
    def _():
        for u in range(2):
            j = step * 2 + u

            def strip_block(i):
                on = identity(BLK) & (col * 16 + j == i)
                total = jnp.where(on, diag_ref[pl.ds(i, 1), :], 0.0)
                for k in range(2):
                    g, h = table_ref[k, 24 + i], table_ref[k, 8 + j]
                    value = strips[2 * u + k][0, jnp.maximum(g, 0), 0]
                    total = total + jnp.where((g >= 0) & (h >= 0), value, 0.0)
                high, low = split(total)
                for part, value in enumerate((high, low, high)):
                    uc[pl.ds(part * TR + i * BLK, BLK), pl.ds(u * BLK, BLK)] = value

            for i in range(8):
                strip_block(i)

        out_ref[...] = dot1(yc[...], uc[...])
        for u in range(2):
            j = step * 2 + u

            def front_block(i):
                for refs, first, count in ((tops, 0, TOP), (bottoms, TOP, BOT)):
                    there = lax.broadcasted_iota(jnp.int32, (count, BLK), 0) + first
                    on = (there == lax.broadcasted_iota(jnp.int32, (count, BLK), 1)) & (
                        col * 16 + j == row * 8 + i
                    )
                    total = jnp.where(on, diag_ref[pl.ds(row * 8 + i, 1), :], 0.0)
                    for k in range(2):
                        g, h = table_ref[k, i], table_ref[k, 8 + j]
                        value = refs[2 * u + k][0, jnp.maximum(g, 0), 0]
                        total = total + jnp.where((g >= 0) & (h >= 0), value, 0.0)
                    at = pl.ds(i * BLK + first, count), pl.ds(u * BLK, BLK)
                    out_ref[at] = total - out_ref[at]

            for i in range(8):
                front_block(i)


def update(table, diag, factors, own, came, strips, recv, rest):
    f32, bf16 = jnp.float32, jnp.bfloat16

    def specs(rows):
        def spec(u, k):
            return pl.BlockSpec(
                (1, 8, 1, rows, BLK), lambda s, table: (k, 0, table[k, 32 + 2 * s + u], 0, 0)
            )

        return [spec(u, k) for u in range(2) for k in range(2)]

    return pl.pallas_call(
        update_kernel,
        out_shape=jax.ShapeDtypeStruct((TR, TC), f32),
        grid_spec=pltpu.PrefetchScalarGridSpec(
            num_scalar_prefetch=1,
            grid=(8,),
            in_specs=[
                pl.BlockSpec((128, BLK), lambda s, table: (0, 0)),
                pl.BlockSpec((TR, 256), lambda s, table: (0, jnp.minimum(s, 3))),
                HBM,
                HBM,
                *specs(BLK),
                *specs(TOP),
                *specs(BOT),
            ],
            out_specs=pl.BlockSpec((TR, 256), lambda s, table: (0, s)),
            scratch_shapes=[
                pltpu.VMEM((TR, TR), f32),
                pltpu.VMEM((TR, 3 * TR), bf16),
                pltpu.VMEM((3 * TR, 256), bf16),
                pltpu.SemaphoreType.DMA,
            ],
        ),
        compiler_params=pltpu.CompilerParams(vmem_limit_bytes=VMEM_LIMIT),
        name="update",
    )(
        table, diag, factors, own, came,
        *[strips.reshape(2, 8, 8, BLK, BLK)] * 4,
        *[recv.reshape(2, 8, 8, TOP, BLK)] * 4,
        *[rest.reshape(2, 8, 8, BOT, BLK)] * 4,
    )


def body(child_blocks, block_map, front_diagonal):
    diag = front_diagonal.reshape(128, BLK)
    send, rest, table = pack(block_map, child_blocks)
    recv, left, strips = exchange(send)
    rest, recv, left, strips = lax.optimization_barrier((rest, recv, left, strips))
    rest = lax.all_to_all(rest, ("row", "col"), split_axis=0, concat_axis=0, tiled=True)
    y, factors = pivots(table, diag, recv, left, strips.reshape(16, 8, BLK, BLK))
    came, strips = spread(y, strips)
    return update(table, diag, factors, y, came, strips, recv, rest)


def solution(mesh):
    return jax.shard_map(
        body,
        mesh=mesh,
        in_specs=(P("row", "col"), P(), P()),
        out_specs=P("row", "col"),
        check_vma=False,
    )
```

```python
import jax
import jax.numpy as jnp
from jax import lax
from jax.experimental import pallas as pl
from jax.experimental.pallas import tpu as pltpu
from jax.sharding import PartitionSpec as P

BLK = 128
PW = 512
TOP = 64
BOT = BLK - TOP
TR = 1024
TC = 2048
MESH = pl.DeviceIdType.MESH
VMEM_LIMIT = 56 * 1024 * 1024
ANY = pl.BlockSpec(memory_space=pl.ANY)
SMEM = pl.BlockSpec(memory_space=pltpu.SMEM)
VMEM = pl.BlockSpec(memory_space=pltpu.VMEM)
HBM = pl.BlockSpec(memory_space=pltpu.HBM)


def pack_kernel(map_ref, child_ref, send_ref, rest_ref, table_ref, sem, rest_sem):
    row, col = lax.axis_index("row"), lax.axis_index("col")
    child, group = row // 8, row % 8

    def start(step, carry):
        t, u = step >> 3, step & 7
        q = map_ref[child, group * 8 + t] >> 4
        c = map_ref[child, col * 8 + u] >> 4
        block = child_ref.at[
            pl.ds(pl.multiple_of(t * BLK, BLK), BLK), pl.ds(pl.multiple_of(u * BLK, BLK), BLK)
        ]
        pltpu.make_async_copy(block, send_ref.at[q * 8 + c], sem).start()
        rest = child_ref.at[
            pl.ds(pl.multiple_of(t * BLK + TOP, 16), BOT), pl.ds(pl.multiple_of(u * BLK, BLK), BLK)
        ]
        pltpu.make_async_copy(rest, rest_ref.at[q * 16 + c], rest_sem).start()
        pltpu.make_async_copy(rest, rest_ref.at[q * 16 + 8 + c], rest_sem).start()
        return carry

    lax.fori_loop(0, 64, start, 0, unroll=8)

    def clear(step, carry):
        table_ref[step // 32, step % 32] = -1
        return carry

    lax.fori_loop(0, 64, clear, 0, unroll=8)

    def look(step, carry):
        k, s = step >> 6, step & 63
        b = map_ref[k, s]

        @pl.when(b >> 3 == row)
        def _():
            table_ref[k, b & 7] = s >> 3

        @pl.when(b >> 4 == col)
        def _():
            table_ref[k, 8 + (b & 15)] = s >> 3

        @pl.when(b < 8)
        def _():
            table_ref[k, 24 + b] = s >> 3

        return carry

    lax.fori_loop(0, 128, look, 0, unroll=8)
    for k in range(2):
        for j in range(16):
            here = table_ref[k, 8 + j]
            before = table_ref[k, 32 + j - 2] if j >= 2 else 0
            table_ref[k, 32 + j] = jnp.where(here >= 0, here, before)
    pltpu.make_async_copy(send_ref, send_ref, sem).wait()
    pltpu.make_async_copy(rest_ref, rest_ref, rest_sem).wait()


def pack(block_map, child):
    return pl.pallas_call(
        pack_kernel,
        out_shape=(
            jax.ShapeDtypeStruct((64, BLK, BLK), jnp.float32),
            jax.ShapeDtypeStruct((128, BOT, BLK), jnp.float32),
            jax.ShapeDtypeStruct((2, 48), jnp.int32),
        ),
        in_specs=[SMEM, VMEM],
        out_specs=(HBM, HBM, SMEM),
        scratch_shapes=[pltpu.SemaphoreType.DMA, pltpu.SemaphoreType.DMA],
        compiler_params=pltpu.CompilerParams(vmem_limit_bytes=VMEM_LIMIT),
        name="pack",
    )(block_map, child)


class Gather:
    def __init__(self, strip_ref, send_sems, recv_sems, first):
        self.strip_ref, self.send_sems, self.recv_sems, self.first = strip_ref, send_sems, recv_sems, first
        self.row, self.col = lax.axis_index("row"), lax.axis_index("col")
        x, y = self.row % 4, self.row // 4
        xl, xr, xo = (x + 3) % 4, (x + 1) % 4, (x + 2) % 4
        yl, yr, yo = (y + 3) % 4, (y + 1) % 4, (y + 2) % 4
        to = {"xr": y * 4 + xr, "xl": y * 4 + xl, "yr": yr * 4 + x, "yl": yl * 4 + x}
        lo, hi = pl.ds(0, 4), pl.ds(4, 4)
        two = [pl.ds(2 * i, 2) for i in range(4)]
        every, left, right = pl.ds(0, 4), pl.ds(0, 2), pl.ds(2, 2)
        self.steps = [
            ((y, x, lo), to["xr"], (y, xl, lo)),
            ((y, x, lo), to["xl"], (y, xr, lo)),
            ((y, x, hi), to["yr"], (yl, x, hi)),
            ((y, x, hi), to["yl"], (yr, x, hi)),
            ((y, xl, two[0]), to["xr"], (y, xo, two[0])),
            ((y, xr, two[1]), to["xl"], (y, xo, two[1])),
            ((yl, x, two[2]), to["yr"], (yo, x, two[2])),
            ((yr, x, two[3]), to["yl"], (yo, x, two[3])),
            ((y, every, lo), to["yr"], (yl, every, lo)),
            ((y, every, lo), to["yl"], (yr, every, lo)),
            ((every, x, hi), to["xr"], (every, xl, hi)),
            ((every, x, hi), to["xl"], (every, xr, hi)),
            ((yl, left, lo), to["yr"], (yo, left, lo)),
            ((yr, right, lo), to["yl"], (yo, right, lo)),
            ((left, xl, hi), to["xr"], (left, xo, hi)),
            ((right, xr, hi), to["xl"], (right, xo, hi)),
        ]

    def copy(self, step, piece, to_row):
        ref = self.strip_ref.at[piece]
        at = step - self.first
        return pltpu.make_async_remote_copy(
            ref, ref, self.send_sems.at[at], self.recv_sems.at[at],
            device_id=(to_row, self.col), device_id_type=MESH,
        )

    def go(self, *steps):
        for step in steps:
            self.copy(step, *self.steps[step][:2]).start()

    def landed(self, *steps):
        for step in steps:
            self.copy(step, self.steps[step][2], self.row).wait_recv()

    def left(self, *steps):
        for step in steps:
            self.copy(step, *self.steps[step][:2]).wait_send()

    def pass_on(self, first):
        for step in range(first, first + 4):
            self.landed(step)
            self.go(step + 4)


def exchange_kernel(
    send_ref, recv_ref, left_ref, strip_ref,
    main_s, main_r, left_s, left_r, col_s, col_r, own_sem, gat_s, gat_r,
):
    row, col = lax.axis_index("row"), lax.axis_index("col")
    me = row * 8 + col
    x, y = row % 4, row // 4
    top, bottom = pl.ds(0, TOP), pl.ds(TOP, BOT)
    own = send_ref.at[(row // 2) * 8 + col]
    own_a = pltpu.make_async_copy(own.at[top], recv_ref.at[me], own_sem.at[0])
    own_b = pltpu.make_async_copy(send_ref.at[col], strip_ref.at[y, x, col], own_sem.at[1])
    own_c = pltpu.make_async_copy(own.at[bottom], left_ref.at[me], own_sem.at[2])

    def send_strip(step, carry):
        to = (col + step) % 8
        pltpu.make_async_remote_copy(
            send_ref.at[to], strip_ref.at[y, x, col], col_s, col_r,
            device_id=(row, to), device_id_type=MESH,
        ).start()
        return carry

    def send_block(step, carry):
        way = (step * 37) % 128
        to_row = ((y + way // 4) % 4) * 4 + (x + way) % 4
        to_col = ((col // 2 + way // 16) % 4) * 2 + (col + way // 64) % 2
        block = send_ref.at[(to_row // 2) * 8 + to_col]
        pltpu.make_async_remote_copy(
            block.at[top], recv_ref.at[me], main_s, main_r,
            device_id=(to_row, to_col), device_id_type=MESH,
        ).start()

        @pl.when(to_col == 0)
        def _():
            pltpu.make_async_remote_copy(
                block.at[bottom], left_ref.at[me], left_s, left_r,
                device_id=(to_row, to_col), device_id_type=MESH,
            ).start()

        return carry

    own_b.start()
    lax.fori_loop(1, 8, send_strip, 0)
    own_a.start()

    @pl.when(col == 0)
    def _():
        own_c.start()

    gather = Gather(strip_ref, gat_s, gat_r, 0)
    lax.fori_loop(1, 17, send_block, 0)
    seven = strip_ref.at[y, x, pl.ds(0, 7)]
    pltpu.make_async_remote_copy(
        seven, seven, col_s, col_r, device_id=(row, col), device_id_type=MESH
    ).wait()
    own_b.wait()
    gather.go(0, 1, 2, 3)
    lax.fori_loop(17, 49, send_block, 0)
    gather.pass_on(0)
    lax.fori_loop(49, 81, send_block, 0)
    gather.landed(4, 5, 6, 7)

    @pl.when(col == 0)
    def _():
        gather.go(8, 9, 10, 11)

    lax.fori_loop(81, 105, send_block, 0)

    @pl.when(col == 0)
    def _():
        gather.pass_on(8)

    lax.fori_loop(105, 128, send_block, 0)
    gather.left(*range(8))

    def blocks(ref, count, send_sem, recv_sem):
        part = ref.at[pl.ds(0, count)]
        return pltpu.make_async_remote_copy(
            part, part, send_sem, recv_sem, device_id=(row, col), device_id_type=MESH
        )

    @pl.when(col == 0)
    def _():
        gather.landed(12, 13, 14, 15)
        gather.left(*range(8, 16))
        own_c.wait()
        blocks(left_ref, 15, left_s, left_r).wait_send()
        blocks(left_ref, 127, left_s, left_r).wait_recv()

    @pl.when(col > 0)
    def _():
        blocks(left_ref, 16, left_s, left_r).wait_send()

    own_a.wait()
    blocks(recv_ref, 127, main_s, main_r).wait()


def exchange(send):
    dma = pltpu.SemaphoreType.DMA
    return pl.pallas_call(
        exchange_kernel,
        out_shape=(
            jax.ShapeDtypeStruct((128, TOP, BLK), jnp.float32),
            jax.ShapeDtypeStruct((128, BOT, BLK), jnp.float32),
            jax.ShapeDtypeStruct((4, 4, 8, BLK, BLK), jnp.float32),
        ),
        in_specs=[HBM],
        out_specs=(HBM, HBM, HBM),
        scratch_shapes=[dma, dma, dma, dma, dma, dma, dma((3,)), dma((16,)), dma((16,))],
        compiler_params=pltpu.CompilerParams(has_side_effects=True, vmem_limit_bytes=VMEM_LIMIT),
        name="exchange",
    )(send)


def split(value):
    high = value.astype(jnp.bfloat16)
    return high, (value - high.astype(jnp.float32)).astype(jnp.bfloat16)


def dot1(a, b):
    return jnp.dot(a, b, preferred_element_type=jnp.float32)


def dot3(a, b):
    return dot1(a[0], b[0]) + (dot1(a[0], b[1]) + dot1(a[1], b[0]))


def identity(n):
    return lax.broadcasted_iota(jnp.int32, (n, n), 0) == lax.broadcasted_iota(jnp.int32, (n, n), 1)


def inverse_into(matrix_ref, scaled_ref, x_ref, out_ref):
    eye = identity(PW)
    matrix = matrix_ref[...]
    diagonal = jnp.where(eye, matrix, 0.0)
    by_col = lax.rsqrt(jnp.sum(diagonal, axis=0, keepdims=True))
    by_row = lax.rsqrt(jnp.sum(diagonal, axis=1, keepdims=True))
    scaled = matrix * by_row * by_col
    scaled_ref[...] = scaled
    bound = jnp.max(jnp.sum(jnp.abs(scaled), axis=0, keepdims=True))
    alpha = jnp.minimum(1.0, 1.9 / bound)

    def begin():
        x_ref[...] = jnp.where(eye, 2.0 * alpha, 0.0) - alpha * alpha * scaled_ref[...]

    def run(most, settled, first, second):
        def step(carry):
            count, _ = carry
            value = x_ref[...]
            residual = jnp.where(eye, 1.0, 0.0) - first(scaled_ref[...], value)
            x_ref[...] += second(value, residual)
            return count + 1, jnp.sum(residual * residual)

        return lax.while_loop(
            lambda carry: (carry[0] < most) & (carry[1] > settled), step, (jnp.int32(0), jnp.float32(1e9))
        )[1]

    def once(a, b):
        return dot1(a.astype(jnp.bfloat16), b.astype(jnp.bfloat16))

    def thrice(a, b):
        return dot3(split(a), split(b))

    begin()
    run(10, 1.0, once, once)
    left = run(5, 1e-6, thrice, once)

    @pl.when(jnp.logical_not(left <= 1e-6))
    def _():
        begin()
        run(48, 1e-6, thrice, thrice)

    residual = jnp.where(eye, 1.0, 0.0) - jnp.dot(
        scaled_ref[...], x_ref[...], precision=lax.Precision.HIGHEST, preferred_element_type=jnp.float32
    )
    value = x_ref[...]
    value = value + thrice(value, residual)
    out_ref[...] = value * by_row * by_col


def pivot_kernel(
    table_ref, diag_ref, recv_ref, left_ref, strip_ref, y_ref, f_ref,
    strips, blocks, piv, tile, inv0, inv1, l10, scaled, newton, schur, sems,
):
    row, col = lax.axis_index("row"), lax.axis_index("col")

    @pl.when(col == 0)
    def _():
        load_a = pltpu.make_async_copy(strip_ref, strips, sems.at[0])
        load_b = pltpu.make_async_copy(recv_ref, blocks.at[:, pl.ds(0, TOP)], sems.at[1])
        load_c = pltpu.make_async_copy(left_ref, blocks.at[:, pl.ds(TOP, BOT)], sems.at[2])
        load_a.start()
        load_b.start()
        load_c.start()
        load_a.wait()

        def pivot_block(step, carry):
            a, b = step // 8, step % 8
            total = jnp.where(identity(BLK) & (a == b), diag_ref[pl.ds(a, 1), :], 0.0)
            for k in range(2):
                ga, gb = table_ref[k, 24 + a], table_ref[k, 24 + b]
                value = strips[k * 8 + jnp.maximum(ga, 0), jnp.maximum(gb, 0)]
                total = total + jnp.where((ga >= 0) & (gb >= 0), value, 0.0)
            piv[pl.ds(pl.multiple_of(a * BLK, BLK), BLK), pl.ds(pl.multiple_of(b * BLK, BLK), BLK)] = total
            return carry

        lax.fori_loop(0, 64, pivot_block, 0)
        schur[...] = piv[:PW, :PW]
        inverse_into(schur, scaled, newton, inv0)
        l10[...] = dot3(split(piv[PW:, :PW]), split(inv0[...]))
        schur[...] = piv[PW:, PW:] - dot3(split(l10[...]), split(piv[:PW, PW:]))

        load_b.wait()
        load_c.wait()

        @pl.when(row == 0)
        def _():
            f_ref[:PW, :] = piv[:PW, :]
            f_ref[PW:, :PW] = l10[...]
            f_ref[PW:, PW:] = schur[...]
            y_ref[...] = jnp.zeros((TR, TR), jnp.float32)
            y_ref[PW:, :PW] = l10[...]

        @pl.when(row > 0)
        def _():
            inverse_into(schur, scaled, newton, inv1)

            def tile_block(step, carry):
                a, b = step // 8, step % 8
                total = jnp.zeros((BLK, BLK), jnp.float32)
                for k in range(2):
                    ga, hb = table_ref[k, a], table_ref[k, 24 + b]
                    value = blocks[k * 64 + jnp.maximum(ga, 0) * 8 + jnp.maximum(hb, 0)]
                    total = total + jnp.where((ga >= 0) & (hb >= 0), value, 0.0)
                tile[pl.ds(pl.multiple_of(a * BLK, BLK), BLK), pl.ds(pl.multiple_of(b * BLK, BLK), BLK)] = total
                return carry

            lax.fori_loop(0, 64, tile_block, 0)
            for part in range(2):
                rows = pl.ds(part * PW, PW)
                factor0 = dot3(split(tile[rows, :PW]), split(inv0[...]))
                f_ref[rows, :PW] = factor0
                rest = tile[rows, PW:] - dot3(split(factor0), split(piv[:PW, PW:]))
                factor1 = dot3(split(rest), split(inv1[...]))
                f_ref[rows, PW:] = factor1
                y_ref[rows, PW:] = factor1
                y_ref[rows, :PW] = f_ref[rows, :PW] - dot3(split(factor1), split(l10[...]))


def pivots(table, diag, recv, left, strips):
    f32 = jnp.float32
    half = pltpu.VMEM((PW, PW), f32)
    return pl.pallas_call(
        pivot_kernel,
        out_shape=(jax.ShapeDtypeStruct((TR, TR), f32), jax.ShapeDtypeStruct((TR, TR), f32)),
        in_specs=[SMEM, VMEM, HBM, HBM, HBM],
        out_specs=(VMEM, VMEM),
        scratch_shapes=[
            pltpu.VMEM((16, 8, BLK, BLK), f32),
            pltpu.VMEM((128, BLK, BLK), f32),
            pltpu.VMEM((TR, TR), f32),
            pltpu.VMEM((TR, TR), f32),
            half, half, half, half, half, half,
            pltpu.SemaphoreType.DMA((3,)),
        ],
        compiler_params=pltpu.CompilerParams(vmem_limit_bytes=VMEM_LIMIT),
        name="pivots",
    )(table, diag, recv, left, strips)


CHUNKS = 16
WINDOW = 4
PASS = 10


def spread_kernel(
    y_ref, _, out_ref, strip_ref, ring_s, ring_r, core_s, core_r, gat_s, gat_r
):
    row, col = lax.axis_index("row"), lax.axis_index("col")
    z, core = col // 2, col % 2
    size = TR // CHUNKS

    def ring(source, t):
        step = 1 if t % 2 == 0 else 3
        rows = pl.ds(t * size, size)
        return pltpu.make_async_remote_copy(
            source.at[rows], out_ref.at[rows], ring_s.at[t], ring_r.at[t],
            device_id=(row, ((z + step) % 4) * 2), device_id_type=MESH,
        )

    def across(source, t):
        rows = pl.ds(t * size, size)
        return pltpu.make_async_remote_copy(
            source.at[rows], out_ref.at[rows], core_s.at[t], core_r.at[t],
            device_id=(row, z * 2 + 1), device_id_type=MESH,
        )

    gather = Gather(strip_ref, gat_s, gat_r, 8)

    @pl.when(col != 0)
    def _():
        gather.go(8, 9, 10, 11)

    @pl.when(col == 0)
    def _():
        for t in range(CHUNKS):
            if t >= WINDOW:
                ring(y_ref, t - WINDOW).wait_send()
            ring(y_ref, t).start()
            across(y_ref, t).start()
        for t in range(CHUNKS):
            if t >= CHUNKS - WINDOW:
                ring(y_ref, t).wait_send()
            across(y_ref, t).wait_send()

    def relay(place):
        def goes(t):
            return place != (3 if t % 2 == 0 else 1)

        order = sorted(range(CHUNKS), key=lambda t: (not goes(t), t))
        for n, t in enumerate(order):
            ring(out_ref, t).wait_recv()
            if goes(t):
                ring(out_ref, t).start()
            across(out_ref, t).start()
            if n == PASS:
                gather.pass_on(8)
        for t in range(CHUNKS):
            if goes(t):
                ring(out_ref, t).wait_send()
            across(out_ref, t).wait_send()

    for place in range(1, 4):

        @pl.when((core == 0) & (z == place))
        def _(place=place):
            relay(place)

    @pl.when(core == 1)
    def _():
        gather.pass_on(8)
        for t in range(CHUNKS):
            across(out_ref, t).wait_recv()

    @pl.when(col != 0)
    def _():
        gather.landed(12, 13, 14, 15)
        gather.left(*range(8, 16))


def spread(y, strips):
    dma = pltpu.SemaphoreType.DMA
    return pl.pallas_call(
        spread_kernel,
        out_shape=(
            jax.ShapeDtypeStruct((TR, TR), jnp.float32),
            jax.ShapeDtypeStruct((4, 4, 8, BLK, BLK), jnp.float32),
        ),
        in_specs=[HBM, HBM],
        out_specs=(HBM, HBM),
        input_output_aliases={1: 1},
        scratch_shapes=[
            dma((CHUNKS,)), dma((CHUNKS,)), dma((CHUNKS,)), dma((CHUNKS,)), dma((8,)), dma((8,)),
        ],
        compiler_params=pltpu.CompilerParams(has_side_effects=True, vmem_limit_bytes=VMEM_LIMIT),
        name="spread",
    )(y, strips)


def update_kernel(table_ref, diag_ref, f_ref, own_ref, came_ref, *refs):
    strips, tops, bottoms = refs[0:4], refs[4:8], refs[8:12]
    out_ref, y, yc, uc, sem = refs[12:]
    row, col = lax.axis_index("row"), lax.axis_index("col")
    step = pl.program_id(0)

    @pl.when(step == 0)
    def _():
        @pl.when(col == 0)
        def _():
            copy = pltpu.make_async_copy(own_ref, y, sem)
            copy.start()
            copy.wait()

        @pl.when(col != 0)
        def _():
            copy = pltpu.make_async_copy(came_ref, y, sem)
            copy.start()
            copy.wait()

        yc[:, :TR], yc[:, 2 * TR :] = split(y[...])
        yc[:, TR : 2 * TR] = yc[:, :TR]

    factors = (col == 0) & (step < 4)

    @pl.when(factors)
    def _():
        out_ref[...] = f_ref[...]

    @pl.when(jnp.logical_not(factors))
    def _():
        for u in range(2):
            j = step * 2 + u

            def strip_block(i):
                on = identity(BLK) & (col * 16 + j == i)
                total = jnp.where(on, diag_ref[pl.ds(i, 1), :], 0.0)
                for k in range(2):
                    g, h = table_ref[k, 24 + i], table_ref[k, 8 + j]
                    value = strips[2 * u + k][0, jnp.maximum(g, 0), 0]
                    total = total + jnp.where((g >= 0) & (h >= 0), value, 0.0)
                high, low = split(total)
                for part, value in enumerate((high, low, high)):
                    uc[pl.ds(part * TR + i * BLK, BLK), pl.ds(u * BLK, BLK)] = value

            for i in range(8):
                strip_block(i)

        out_ref[...] = dot1(yc[...], uc[...])
        for u in range(2):
            j = step * 2 + u

            def front_block(i):
                for refs, first, count in ((tops, 0, TOP), (bottoms, TOP, BOT)):
                    there = lax.broadcasted_iota(jnp.int32, (count, BLK), 0) + first
                    on = (there == lax.broadcasted_iota(jnp.int32, (count, BLK), 1)) & (
                        col * 16 + j == row * 8 + i
                    )
                    total = jnp.where(on, diag_ref[pl.ds(row * 8 + i, 1), :], 0.0)
                    for k in range(2):
                        g, h = table_ref[k, i], table_ref[k, 8 + j]
                        value = refs[2 * u + k][0, jnp.maximum(g, 0), 0]
                        total = total + jnp.where((g >= 0) & (h >= 0), value, 0.0)
                    at = pl.ds(i * BLK + first, count), pl.ds(u * BLK, BLK)
                    out_ref[at] = total - out_ref[at]

            for i in range(8):
                front_block(i)


def update(table, diag, factors, own, came, strips, recv, rest):
    f32, bf16 = jnp.float32, jnp.bfloat16

    def specs(rows):
        def spec(u, k):
            return pl.BlockSpec(
                (1, 8, 1, rows, BLK), lambda s, table: (k, 0, table[k, 32 + 2 * s + u], 0, 0)
            )

        return [spec(u, k) for u in range(2) for k in range(2)]

    return pl.pallas_call(
        update_kernel,
        out_shape=jax.ShapeDtypeStruct((TR, TC), f32),
        grid_spec=pltpu.PrefetchScalarGridSpec(
            num_scalar_prefetch=1,
            grid=(8,),
            in_specs=[
                pl.BlockSpec((128, BLK), lambda s, table: (0, 0)),
                pl.BlockSpec((TR, 256), lambda s, table: (0, jnp.minimum(s, 3))),
                HBM,
                HBM,
                *specs(BLK),
                *specs(TOP),
                *specs(BOT),
            ],
            out_specs=pl.BlockSpec((TR, 256), lambda s, table: (0, s)),
            scratch_shapes=[
                pltpu.VMEM((TR, TR), f32),
                pltpu.VMEM((TR, 3 * TR), bf16),
                pltpu.VMEM((3 * TR, 256), bf16),
                pltpu.SemaphoreType.DMA,
            ],
        ),
        compiler_params=pltpu.CompilerParams(vmem_limit_bytes=VMEM_LIMIT),
        name="update",
    )(
        table, diag, factors, own, came,
        *[strips.reshape(2, 8, 8, BLK, BLK)] * 4,
        *[recv.reshape(2, 8, 8, TOP, BLK)] * 4,
        *[rest.reshape(2, 8, 8, BOT, BLK)] * 4,
    )


def body(child_blocks, block_map, front_diagonal):
    diag = front_diagonal.reshape(128, BLK)
    send, rest, table = pack(block_map, child_blocks)
    recv, left, strips = exchange(send)
    rest, recv, left, strips = lax.optimization_barrier((rest, recv, left, strips))
    rest = lax.all_to_all(rest, ("row", "col"), split_axis=0, concat_axis=0, tiled=True)
    y, factors = pivots(table, diag, recv, left, strips.reshape(16, 8, BLK, BLK))
    came, strips = spread(y, strips)
    return update(table, diag, factors, y, came, strips, recv, rest)


def solution(mesh):
    return jax.shard_map(
        body,
        mesh=mesh,
        in_specs=(P("row", "col"), P(), P()),
        out_specs=P("row", "col"),
        check_vma=False,
    )
```
